32 devices in a mesh: groups: 2 (over x), expert: 8 (over z, y), tensor: 2 (over core).
Axes of the slice: x: 2, y: 2, z: 4, core: 2. Of those that a mesh axis runs over, the one named last changes fastest.
Arguments:
- tokens: bfloat16 [4096, 3584], P(('groups', 'expert', 'tensor')), parts along dimension 0, may hold values from -6 to 6
- router_weight: bfloat16 [256, 3584], P('expert'), may hold values from -0.09375 to 0.09375
- gate_weight: bfloat16 [8, 3584, 1024], P('expert', None, 'tensor'), may hold values from -0.09375 to 0.09375
- up_weight: bfloat16 [8, 3584, 1024], P('expert', None, 'tensor'), may hold values from -0.09375 to 0.09375
- down_weight: bfloat16 [8, 1024, 3584], P('expert', 'tensor'), may hold values from -0.1875 to 0.1875
- policy_logits: float32 [4096, 256], P(('groups', 'expert', 'tensor')), parts along dimension 0, may hold values from -18 to 18
- expert_ids: int32 [4096, 8], P(('groups', 'expert', 'tensor')), parts along dimension 0, may hold values from 0 to 255, as said below
- slots: int32 [4096, 8], P(('groups', 'expert', 'tensor')), parts along dimension 0, may hold values from 0 to 8, as said below
- occupancy: int32 [8, 32], P('expert', 'groups'), parts along dimension 1, may hold values from 0 to 8, as said below
- env_mask: int32 [4096], P(('groups', 'expert', 'tensor')), parts along dimension 0, may hold values 0 or 1
Outputs:
- mixed: bfloat16 [4096, 3584], P(('groups', 'expert', 'tensor')), parts along dimension 0
- kl_terms: float32 [4096], P(('groups', 'expert', 'tensor')), parts along dimension 0
The draws below stay inside these ranges and needn't reach their ends.
There are 2 independent parts, one for each index of `groups`. The reference program is written for one: setup_inputs(seed, part) draws one part's arguments, and reference() takes and returns one part's arrays. A program takes and returns all parts, laid end to end along the dimension named above; an argument that names none is the same for every part. Nothing has to cross between parts.
Inputs may be any that keep to these rules, and one draw needn't show every extreme that they name: `expert_ids`: each row holds 8 different expert numbers; numbers below 8 are the experts held in this window. For a choice of a window expert that is placed, its slot among the 8 slots of its source device and expert; the placed choices of one source and expert hold the slots 0, 1, 2 and so on in order of token, then choice; 8 marks a choice that is not placed (expert outside the window or buffer full). occupancy[e, s] is the number of placed choices of source device s for window expert e; some expert is full from every source.
All inputs are finite; a program needn't handle non-finite values. No bound on the sum of `env_mask` on one device may be relied on, other than what follows from the above.
Results may differ from the reference program's by a relative error of at most 0.0074.
Values may be sent and summed in bfloat16 or wider, within the bound.
No kernel may reach another device: no remote copies, remote signals or barrier semaphores. Data moves between devices by JAX's collectives and lax.ppermute only.
A program may use at most 64 MiB of HBM per device.

```python
import jax
import jax.numpy as jnp
from jax import lax

D = 3584
FF = 1024
EXPERTS_ALL = 256
TOP = 8
TOK_DEV = 128
CAP = 8
EXPERTS = 8
SOURCES = 16
TOKENS = 2048
N_TENSOR = 2


def routing(key):
    keys = jax.random.split(key, 5)
    base = jax.random.randint(keys[0], (TOKENS, EXPERTS_ALL), 0, 65536, dtype=jnp.int32)
    favour = jax.random.randint(keys[1], (EXPERTS_ALL,), 0, 4, dtype=jnp.int32) * 16384
    common = jax.random.randint(keys[2], (), 0, EXPERTS, dtype=jnp.int32)
    local_hot = jax.random.randint(keys[3], (SOURCES,), 0, EXPERTS, dtype=jnp.int32)

    def shuffled(block_key):
        return jax.random.permutation(block_key, TOK_DEV).astype(jnp.int32)
    ranks = jax.vmap(shuffled)(jax.random.split(keys[4], SOURCES)).reshape(TOKENS)
    columns = jnp.arange(EXPERTS_ALL, dtype=jnp.int32)
    hot_rows = jnp.repeat(local_hot, TOK_DEV)
    push_common = (ranks < 2 * CAP)[:, None] & (columns[None, :] == common)
    push_local = ((ranks >= 2 * CAP) & (ranks < 3 * CAP))[:, None] & (columns[None, :] == hot_rows[:, None])
    scores = base + favour[None, :] + 524288 * (push_common | push_local).astype(jnp.int32)
    scores = scores * EXPERTS_ALL + columns[None, :]
    expert_ids = lax.top_k(scores, TOP)[1].astype(jnp.int32)
    window = jnp.arange(EXPERTS, dtype=jnp.int32)
    hits = (expert_ids[:, :, None] == window[None, None, :]).astype(jnp.int32).reshape(SOURCES, TOK_DEV * TOP, EXPERTS)
    before = jnp.cumsum(hits, axis=1) - hits
    rank = jnp.sum(hits * before, axis=2).reshape(TOKENS, TOP)
    inside = expert_ids < EXPERTS
    slots = jnp.where(inside & (rank < CAP), rank, CAP).astype(jnp.int32)
    occupancy = jnp.minimum(jnp.sum(hits, axis=1), CAP).T.astype(jnp.int32)
    return (expert_ids, slots, occupancy)


def draw_expert_ids(key, part):
    return routing(key)[0]


def draw_slots(key, part):
    return routing(key)[1]


def draw_occupancy(key, part):
    return routing(key)[2]


def touch_ends(array, own_key, least, top_value):
    spot = [jax.random.randint(jax.random.fold_in(own_key, axis), (), 0, length) for axis, length in enumerate(array.shape)]
    widest = array.shape.index(max(array.shape))
    beside = spot[:widest] + [(spot[widest] + 1) % array.shape[widest]] + spot[widest + 1:]
    return array.at[tuple(spot)].set(least).at[tuple(beside)].set(top_value)


def steps_of(stream_key, shape, shards, least, largest):
    def one(axis_at, parts):
        heights = jax.random.uniform(jax.random.fold_in(jax.random.fold_in(stream_key, 6), axis_at), (parts,), jnp.float32, least / len(shards), largest / len(shards))
        return jnp.repeat(jnp.exp(heights), shape[axis_at] // parts).reshape((-1,) + (1,) * (len(shape) - axis_at - 1))

    level = one(*shards[0])
    for cut in shards[1:]:
        level = level * one(*cut)
    return level


def normal_values(key, shape, deviation, limit, cuts=(), kind=jnp.bfloat16):
    result = jax.random.normal(key, shape, jnp.float32) * deviation
    if len(cuts) > 0:
        result = steps_of(key, shape, cuts, -0.22, 0.18) * result
    return jnp.clip(result, min=-limit, max=limit).astype(kind)


def setup_inputs(seed: int = 0, part: int = 0) -> dict:
    key_list = jax.random.split(jax.random.key(seed), 11)
    part_splits = jax.random.split(jax.random.fold_in(key_list[10], part), 11)
    tokens = normal_values(part_splits[0], (TOKENS, D), 1.0, 6.0, ((0, 16),))
    router_weight = normal_values(key_list[1], (EXPERTS_ALL, D), D ** -0.5, 0.09375, ((0, 8),))
    gate_weight = normal_values(key_list[2], (EXPERTS, D, FF), D ** -0.5, 0.09375, ((0, 8), (2, 2)))
    up_weight = normal_values(key_list[3], (EXPERTS, D, FF), D ** -0.5, 0.09375, ((0, 8), (2, 2)))
    down_weight = normal_values(key_list[4], (EXPERTS, FF, D), FF ** -0.5, 0.1875, ((0, 8), (1, 2)))
    policy_logits = normal_values(part_splits[5], (TOKENS, EXPERTS_ALL), 3.0, 18.0, ((0, 16),), jnp.float32)
    expert_ids = draw_expert_ids(jax.random.fold_in(jax.random.fold_in(key_list[10], part), 71), part)
    slots = draw_slots(jax.random.fold_in(jax.random.fold_in(key_list[10], part), 71), part)
    occupancy = draw_occupancy(jax.random.fold_in(jax.random.fold_in(key_list[10], part), 71), part)
    env_mask = touch_ends((jax.random.randint(part_splits[9], (TOKENS,), 0, 3) < 1).astype(jnp.int32), jax.random.fold_in(part_splits[9], 1), 0, 1)
    return {"tokens": tokens, "router_weight": router_weight, "gate_weight": gate_weight, "up_weight": up_weight, "down_weight": down_weight, "policy_logits": policy_logits, "expert_ids": expert_ids, "slots": slots, "occupancy": occupancy, "env_mask": env_mask}


def placements(expert_ids, slots, count, capacity):
    valid = (expert_ids < count) & (slots < capacity)
    return jnp.where(valid, expert_ids * capacity + slots, -1).astype(jnp.int32)


def select_matrix(place, width):
    columns = jnp.arange(width, dtype=jnp.int32)
    hits = place[:, :, None] == columns[None, None, :]
    return jnp.any(hits, axis=1).astype(jnp.bfloat16)


def weighted_matrix(place, weights, width):
    columns = jnp.arange(width, dtype=jnp.int32)
    hits = place[:, :, None] == columns[None, None, :]
    picked = jnp.where(hits, weights[:, :, None], jnp.zeros((), jnp.bfloat16))
    return jnp.sum(picked, axis=1).astype(jnp.bfloat16)


def router_terms(logits, policy_logits, expert_ids, env_mask):
    scores = jax.nn.sigmoid(logits)
    chosen = jnp.take_along_axis(scores, expert_ids, axis=1)
    combine_weights = (2.5 * chosen / jnp.sum(chosen, axis=1, keepdims=True)).astype(jnp.bfloat16)
    log_p = jax.nn.log_sigmoid(logits) - jnp.log(jnp.sum(scores, axis=1, keepdims=True))
    policy = jax.nn.sigmoid(policy_logits)
    log_q = jax.nn.log_sigmoid(policy_logits) - jnp.log(jnp.sum(policy, axis=1, keepdims=True))
    keep = (1 - env_mask).astype(jnp.float32)
    kl_terms = keep * jnp.sum(jnp.exp(log_q) * (log_q - log_p), axis=1)
    return combine_weights, kl_terms


def reference(tokens, router_weight, gate_weight, up_weight, down_weight, policy_logits, expert_ids, slots, occupancy, env_mask):
    logits = lax.dot_general(tokens, router_weight, (((1,), (1,)), ((), ())), preferred_element_type=jnp.float32)
    combine_weights, kl_terms = router_terms(logits, policy_logits, expert_ids, env_mask)
    place = placements(expert_ids, slots, EXPERTS, CAP)
    width = EXPERTS * CAP

    def dispatch_one(operands):
        block_tokens, block_place = operands
        matrix = select_matrix(block_place, width)
        return lax.dot_general(matrix, block_tokens, (((0,), (0,)), ((), ())), preferred_element_type=jnp.float32).astype(jnp.bfloat16)

    sent = lax.map(dispatch_one, (tokens.reshape(SOURCES, TOK_DEV, D), place.reshape(SOURCES, TOK_DEV, TOP)))
    rows_in = sent.reshape(SOURCES, EXPERTS, CAP, D).transpose(1, 0, 2, 3).reshape(EXPERTS, SOURCES * CAP, D)
    capacity_iota = jnp.arange(CAP, dtype=jnp.int32)
    alive = (capacity_iota[None, None, :] < occupancy[:, :, None]).reshape(EXPERTS, SOURCES * CAP)
    share = FF // N_TENSOR

    def expert_one(operands):
        rows, living, w_gate, w_up, w_down = operands
        gate = jnp.dot(rows, w_gate, preferred_element_type=jnp.float32)
        up = jnp.dot(rows, w_up, preferred_element_type=jnp.float32)
        hidden = jnp.where(living[:, None], jax.nn.silu(gate) * up, jnp.zeros((), jnp.float32)).astype(jnp.bfloat16)
        total = jnp.zeros((rows.shape[0], D), jnp.float32)
        for index in range(N_TENSOR):
            partial_value = jnp.dot(hidden[:, index * share:(index + 1) * share], w_down[index * share:(index + 1) * share], preferred_element_type=jnp.float32)
            partial_value = lax.optimization_barrier(partial_value.astype(jnp.bfloat16))
            total = total + partial_value.astype(jnp.float32)
        return total.astype(jnp.bfloat16)

    expert_out = lax.map(expert_one, (rows_in, alive, gate_weight, up_weight, down_weight))
    back = expert_out.reshape(EXPERTS, SOURCES, CAP, D).transpose(1, 0, 2, 3).reshape(SOURCES, width, D)

    def combine_one(operands):
        block_back, block_place, block_weights = operands
        matrix = weighted_matrix(block_place, block_weights, width)
        return jnp.dot(matrix, block_back, preferred_element_type=jnp.float32).astype(jnp.bfloat16)

    mixed = lax.map(combine_one, (back, place.reshape(SOURCES, TOK_DEV, TOP), combine_weights.reshape(SOURCES, TOK_DEV, TOP)))
    return mixed.reshape(TOKENS, D), kl_terms
```

```python
import jax
import jax.numpy as jnp
from jax import lax
from jax.sharding import PartitionSpec as P

CAP = 8
SWAP = [(0, 1), (1, 0)]


def swap_cores(value):
    return lax.ppermute(value, "tensor", SWAP)


def across(value, axis, distance):
    size = lax.axis_size(axis)
    return lax.ppermute(value, axis, [(s, s ^ distance) for s in range(size)])


def placed_columns(expert_ids, slots, count):
    valid = (expert_ids < count) & (slots < CAP)
    return jnp.where(valid, expert_ids * CAP + slots, -1)


def select_matrix(place, width):
    columns = jnp.arange(width, dtype=jnp.int32)
    hits = place[:, :, None] == columns[None, None, :]
    return jnp.any(hits, axis=1).astype(jnp.bfloat16)


def weighted_matrix(place, weights, width):
    columns = jnp.arange(width, dtype=jnp.int32)
    hits = place[:, :, None] == columns[None, None, :]
    picked = jnp.where(hits, weights[:, :, None], jnp.zeros((), jnp.bfloat16))
    return jnp.sum(picked, axis=1)


def router_terms(logits, policy_logits, expert_ids, env_mask):
    scores = jax.nn.sigmoid(logits)
    columns = jnp.arange(logits.shape[1], dtype=jnp.int32)
    chosen = jnp.stack(
        [
            jnp.sum(jnp.where(expert_ids[:, k : k + 1] == columns[None, :], scores, 0.0), axis=1)
            for k in range(expert_ids.shape[1])
        ],
        axis=1,
    )
    combine_weights = (2.5 * chosen / jnp.sum(chosen, axis=1, keepdims=True)).astype(jnp.bfloat16)
    log_p = jax.nn.log_sigmoid(logits) - jnp.log(jnp.sum(scores, axis=1, keepdims=True))
    policy = jax.nn.sigmoid(policy_logits)
    log_q = jax.nn.log_sigmoid(policy_logits) - jnp.log(jnp.sum(policy, axis=1, keepdims=True))
    keep = (1 - env_mask).astype(jnp.float32)
    kl_terms = keep * jnp.sum(jnp.exp(log_q) * (log_q - log_p), axis=1)
    return (combine_weights, kl_terms)


def dot_rows(left, right):
    return lax.dot_general(
        left, right, (((1,), (1,)), ((), ())), preferred_element_type=jnp.float32
    )


def z_pieces(piece):
    z = lax.axis_index("expert") // 2
    got = [piece] + [across(piece, "expert", 2 * d) for d in (1, 2, 3)]
    out = jnp.zeros((4,) + piece.shape, piece.dtype)
    for d in range(4):
        out = lax.dynamic_update_index_in_dim(out, got[d], z ^ d, 0)
    return out


def per_device(
    tokens,
    router_weight,
    gate_weight,
    up_weight,
    down_weight,
    policy_logits,
    expert_ids,
    slots,
    occupancy,
    env_mask,
):
    experts = lax.axis_size("expert")
    groups = lax.axis_size("groups")
    pairs = lax.axis_size("tensor")
    core = lax.axis_index("tensor")
    model_width = tokens.shape[1]
    width = experts * CAP
    staged = experts == 8 and groups == 2 and pairs == 2
    half = model_width // 2
    if staged:
        group = lax.axis_index("groups")
        quarter = half // 2
        piece = lax.dynamic_slice_in_dim(router_weight, core * half + group * quarter, quarter, axis=1)
        level_z = z_pieces(piece)
        peer_tokens = swap_cores(lax.dynamic_slice_in_dim(tokens, (1 - core) * half, half, axis=1))
    place = placed_columns(expert_ids, slots, experts)
    matrix = select_matrix(place, width)
    outgoing = lax.dot_general(
        matrix, tokens, (((0,), (0,)), ((), ())), preferred_element_type=jnp.float32
    )
    outgoing = outgoing.astype(jnp.bfloat16).reshape(experts, CAP, model_width)
    arrived = lax.all_to_all(outgoing, "expert", split_axis=0, concat_axis=0, tiled=True)
    arrived = arrived.reshape(-1, model_width)
    if staged:
        level_y = across(level_z, "expert", 1)
        level_x = across(level_z, "groups", 1)
        level_xy = across(level_y, "groups", 1)

    used = occupancy[0].reshape(experts, pairs)
    used = jnp.stack(
        [jnp.take(used, core, axis=1), jnp.take(used, 1 - core, axis=1)], axis=0
    ).reshape(-1)
    alive = (jnp.arange(CAP, dtype=jnp.int32)[None, :] < used[:, None]).reshape(-1)
    rows = jnp.concatenate([arrived, swap_cores(arrived)], axis=0)
    gate = jnp.dot(rows, gate_weight[0], preferred_element_type=jnp.float32)
    up = jnp.dot(rows, up_weight[0], preferred_element_type=jnp.float32)
    hidden = jnp.where(alive[:, None], jax.nn.silu(gate) * up, jnp.zeros((), jnp.float32)).astype(
        jnp.bfloat16
    )
    partial_value = jnp.dot(hidden, down_weight[0], preferred_element_type=jnp.float32).astype(
        jnp.bfloat16
    )
    other = swap_cores(partial_value[width:])
    summed = (partial_value[:width].astype(jnp.float32) + other.astype(jnp.float32)).astype(jnp.bfloat16)
    returned = lax.all_to_all(
        summed.reshape(experts, CAP, model_width), "expert", split_axis=0, concat_axis=0, tiled=True
    )
    if staged:
        y = lax.axis_index("expert") % 2

        def in_order(own, other):
            return jnp.where(
                y == 0, jnp.stack([own, other], axis=1), jnp.stack([other, own], axis=1)
            ).reshape(-1, quarter)

        mine = in_order(level_z, level_y)
        theirs = in_order(level_x, level_xy)
        at_mine = group * quarter
        at_theirs = (1 - group) * quarter
        own_tokens = lax.dynamic_slice_in_dim(tokens, core * half, half, axis=1)

        def half_logits(value):
            first = lax.dynamic_slice_in_dim(value, at_mine, quarter, axis=1)
            second = lax.dynamic_slice_in_dim(value, at_theirs, quarter, axis=1)
            return dot_rows(first, mine) + dot_rows(second, theirs)

        logits = half_logits(own_tokens) + swap_cores(half_logits(peer_tokens))
    else:
        logits = dot_rows(tokens, lax.all_gather(router_weight, "expert", axis=0, tiled=True))
    combine_weights, kl_terms = router_terms(logits, policy_logits, expert_ids, env_mask)
    combine_matrix = weighted_matrix(place, combine_weights, width)
    mixed = jnp.dot(
        combine_matrix, returned.reshape(width, model_width), preferred_element_type=jnp.float32
    ).astype(jnp.bfloat16)
    return (mixed, kl_terms)


def solution(mesh):
    in_specs = (
        P(("groups", "expert", "tensor"), None),
        P("expert", None),
        P("expert", None, "tensor"),
        P("expert", None, "tensor"),
        P("expert", "tensor", None),
        P(("groups", "expert", "tensor"), None),
        P(("groups", "expert", "tensor"), None),
        P(("groups", "expert", "tensor"), None),
        P("expert", "groups"),
        P(("groups", "expert", "tensor")),
    )
    out_specs = (P(("groups", "expert", "tensor"), None), P(("groups", "expert", "tensor")))
    return jax.shard_map(
        per_device, mesh=mesh, in_specs=in_specs, out_specs=out_specs, check_vma=False
    )
```

```python
import functools

import jax
import jax.numpy as jnp
from jax import lax
from jax.experimental import pallas as pl
from jax.experimental.pallas import tpu as pltpu
from jax.sharding import PartitionSpec as P

CAP = 8
SWAP = [(0, 1), (1, 0)]
WHOLE = pl.BlockSpec(memory_space=pltpu.VMEM)
LEFT = pl.BlockSpec(memory_space=pltpu.HBM)


def swap_cores(value):
    return lax.ppermute(value, "tensor", SWAP)


def across(value, axis, distance):
    size = lax.axis_size(axis)
    return lax.ppermute(value, axis, [(s, s ^ distance) for s in range(size)])


def dot_rows(left, right):
    return lax.dot_general(
        left, right, (((1,), (1,)), ((), ())), preferred_element_type=jnp.float32
    )


def dot_columns(left, right):
    return lax.dot_general(
        left, right, (((0,), (0,)), ((), ())), preferred_element_type=jnp.float32
    )


def params(mib):
    return pltpu.CompilerParams(vmem_limit_bytes=mib << 20)


def cost(flops, nbytes):
    return pl.CostEstimate(flops=flops, bytes_accessed=nbytes, transcendentals=0)


def buffer_hits(ids, slots, width):
    choices, tokens = ids.shape
    valid = (ids < width // CAP) & (slots < CAP)
    place = jnp.where(valid, ids * CAP + slots, -1)
    rows = lax.broadcasted_iota(jnp.int32, (width, tokens), 0)
    hits = rows == place[0:1, :]
    for k in range(1, choices):
        hits = hits | (rows == place[k : k + 1, :])
    return hits


def masked_hidden(g, u, occupancy, side):
    count = g.shape[0]
    sources = occupancy.shape[1]
    row = lax.broadcasted_iota(jnp.int32, (count, sources), 0)
    column = lax.broadcasted_iota(jnp.int32, (count, sources), 1)
    here = column == row // CAP * 2 + side
    used = jnp.sum(jnp.where(here, occupancy[...], 0), axis=1, keepdims=True)
    live = row[:, 0:1] % CAP < used
    return jnp.where(live, g / (1.0 + jnp.exp(-g)) * u, 0.0).astype(jnp.bfloat16)


def near_kernel(parts, own, occupancy, gate, up, down, w_gate, w_up, w_down, hidden, sems):
    depth = own.shape[1] // parts
    copies = []
    for part in range(parts):
        at = pl.ds(part * depth, depth)
        copies.append(pltpu.make_async_copy(gate.at[:, at, :], w_gate.at[:, at, :], sems.at[0, part]))
        copies.append(pltpu.make_async_copy(up.at[:, at, :], w_up.at[:, at, :], sems.at[1, part]))
    last = pltpu.make_async_copy(down, w_down, sems.at[2, 0])
    for copy in copies + [last]:
        copy.start()
    g = u = 0.0
    for part in range(parts):
        at = slice(part * depth, (part + 1) * depth)
        rows = own[:, at]
        copies[2 * part].wait()
        g = g + jnp.dot(rows, w_gate[0, at, :], preferred_element_type=jnp.float32)
        copies[2 * part + 1].wait()
        u = u + jnp.dot(rows, w_up[0, at, :], preferred_element_type=jnp.float32)
    hidden[...] = masked_hidden(g, u, occupancy, lax.axis_index("tensor"))
    last.wait()


def ffn_near(own, occupancy, gate, up, down):
    count, model_width = own.shape
    hidden_width = gate.shape[2]
    parts = 4 if model_width % 512 == 0 else 1
    weights = [pltpu.with_memory_space_constraint(w, pltpu.HBM) for w in (gate, up, down)]
    return pl.pallas_call(
        functools.partial(near_kernel, parts),
        out_shape=tuple(jax.ShapeDtypeStruct(w.shape, w.dtype) for w in (gate, up, down))
        + (jax.ShapeDtypeStruct((count, hidden_width), own.dtype),),
        in_specs=[WHOLE, WHOLE, LEFT, LEFT, LEFT],
        out_specs=(WHOLE,) * 4,
        scratch_shapes=[pltpu.SemaphoreType.DMA((3, parts))],
        compiler_params=params(16),
        cost_estimate=cost(4 * count * model_width * hidden_width, 2 * count * model_width),
        name="ffn_near",
    )(own, occupancy, *weights)


def far_kernel(parts, peer, occupancy, own_hidden, gate, up, down, out_own, out_peer):
    count = peer.shape[0]
    wide = down.shape[2] // parts
    g = jnp.dot(peer[...], gate[0], preferred_element_type=jnp.float32)
    u = jnp.dot(peer[...], up[0], preferred_element_type=jnp.float32)
    far = masked_hidden(g, u, occupancy, 1 - lax.axis_index("tensor"))
    hidden = jnp.concatenate([own_hidden[...], far], axis=0)
    for part in range(parts):
        at = slice(part * wide, (part + 1) * wide)
        value = jnp.dot(hidden, down[0, :, at], preferred_element_type=jnp.float32)
        value = value.astype(jnp.bfloat16)
        out_own[:, at] = value[:count]
        out_peer[:, at] = value[count:]


def ffn_far(peer, occupancy, own_hidden, gate, up, down):
    half = jax.ShapeDtypeStruct(peer.shape, peer.dtype)
    count, model_width = peer.shape
    hidden_width = gate.shape[2]
    parts = 4 if model_width % 512 == 0 else 1
    return pl.pallas_call(
        functools.partial(far_kernel, parts),
        out_shape=(half, half),
        in_specs=[WHOLE] * 6,
        out_specs=(WHOLE, WHOLE),
        compiler_params=params(16),
        cost_estimate=cost(8 * count * model_width * hidden_width, 2 * count * model_width),
        name="ffn_far",
    )(peer, occupancy, own_hidden, gate, up, down)


def add_kernel(ours, other, out):
    out[...] = (ours[...].astype(jnp.float32) + other[...].astype(jnp.float32)).astype(out.dtype)


def add_halves(ours, other):
    return pl.pallas_call(
        add_kernel,
        out_shape=jax.ShapeDtypeStruct(ours.shape, ours.dtype),
        in_specs=[WHOLE] * 2,
        out_specs=WHOLE,
        compiler_params=params(16),
        cost_estimate=cost(ours.size, 6 * ours.size),
        name="add_halves",
    )(ours, other)


def logits_kernel(place, own_tokens, peer_tokens, level, level_y, level_x, level_xy, out_own, out_peer):
    z, y, near = place[0], place[1], place[2]
    quarter = level.shape[1]
    depth = level.shape[0] // 4
    ends = [pl.multiple_of(near * quarter, 128), pl.multiple_of((1 - near) * quarter, 128)]
    for tokens, out in ((own_tokens, out_own), (peer_tokens, out_peer)):
        first = tokens[:, pl.ds(ends[0], quarter)]
        second = tokens[:, pl.ds(ends[1], quarter)]
        for side, (left, right) in enumerate(((level, level_x), (level_y, level_xy))):
            value = dot_rows(left[...], first) + dot_rows(right[...], second)
            for d in range(4):
                expert = 2 * (z ^ d) + (y ^ side)
                at = pl.ds(pl.multiple_of(expert * depth, depth), depth)
                out[at, :] = value[d * depth : (d + 1) * depth]


def half_logits(place, own_tokens, peer_tokens, *levels):
    rows = 2 * levels[0].shape[0]
    count, half = own_tokens.shape
    out = jax.ShapeDtypeStruct((rows, count), jnp.float32)
    return pl.pallas_call(
        logits_kernel,
        out_shape=(out, out),
        in_specs=[pl.BlockSpec(memory_space=pltpu.SMEM)] + [WHOLE] * 6,
        out_specs=(WHOLE, WHOLE),
        compiler_params=params(16),
        cost_estimate=cost(4 * rows * count * half, 2 * half * (rows + 2 * count)),
        name="half_logits",
    )(place, own_tokens, peer_tokens, *levels)


def log_sigmoid(value):
    return jnp.minimum(value, 0.0) - jnp.log1p(jnp.exp(-jnp.abs(value)))


def terms_kernel(ids, slots, mask, policy, *refs):
    parts, (weights, kl) = refs[:-2], refs[-2:]
    logits = parts[0][...]
    for part in parts[1:]:
        logits = logits + part[...]
    experts, tokens = logits.shape
    width = weights.shape[0]
    window = width // CAP
    scores = 1.0 / (1.0 + jnp.exp(-logits))
    names = lax.broadcasted_iota(jnp.int32, (experts, tokens), 0)
    choices = ids[...]
    chosen = jnp.zeros((experts, tokens), jnp.float32)
    for k in range(choices.shape[0]):
        chosen = chosen + jnp.where(names == choices[k : k + 1, :], scores, 0.0)
    total = jnp.sum(chosen, axis=0, keepdims=True)
    shares = (2.5 * scores[:window] / total).astype(jnp.bfloat16).astype(jnp.float32)
    spread = jnp.broadcast_to(shares[:, None, :], (window, CAP, tokens)).reshape(width, tokens)
    hits = buffer_hits(choices, slots[...], width)
    weights[...] = jnp.where(hits, spread, 0.0).astype(jnp.bfloat16)
    log_p = log_sigmoid(logits) - jnp.log(jnp.sum(scores, axis=0, keepdims=True))
    q = policy[...]
    policy_scores = 1.0 / (1.0 + jnp.exp(-q))
    log_q = log_sigmoid(q) - jnp.log(jnp.sum(policy_scores, axis=0, keepdims=True))
    keep = (1 - mask[...]).astype(jnp.float32)
    kl[...] = keep * jnp.sum(jnp.exp(log_q) * (log_q - log_p), axis=0, keepdims=True)


def router_terms(ids, slots, mask, policy, parts, width):
    experts, tokens = policy.shape
    return pl.pallas_call(
        terms_kernel,
        out_shape=(
            jax.ShapeDtypeStruct((width, tokens), jnp.bfloat16),
            jax.ShapeDtypeStruct((1, tokens), jnp.float32),
        ),
        in_specs=[WHOLE] * (4 + len(parts)),
        out_specs=(WHOLE, WHOLE),
        compiler_params=params(16),
        cost_estimate=cost(30 * experts * tokens, 12 * experts * tokens),
        name="router_terms",
    )(ids, slots, mask, policy, *parts)


def per_device(
    tokens,
    router_weight,
    gate_weight,
    up_weight,
    down_weight,
    policy_logits,
    expert_ids,
    slots,
    occupancy,
    env_mask,
):
    experts = lax.axis_size("expert")
    groups = lax.axis_size("groups")
    core = lax.axis_index("tensor")
    model_width = tokens.shape[1]
    width = experts * CAP
    half = model_width // 2
    staged = experts == 8 and groups == 2
    ids, slots = expert_ids.T, slots.T

    hits = buffer_hits(ids, slots, width)
    outgoing = jnp.dot(hits.astype(jnp.bfloat16), tokens, preferred_element_type=jnp.float32)
    outgoing = outgoing.astype(jnp.bfloat16).reshape(experts, CAP, model_width)
    arrived = lax.all_to_all(outgoing, "expert", split_axis=0, concat_axis=0, tiled=True)
    arrived = arrived.reshape(width, model_width)
    if staged:
        group, at = lax.axis_index("groups"), lax.axis_index("expert")
        quarter = half // 2
        piece = lax.dynamic_slice_in_dim(router_weight, core * half + group * quarter, quarter, axis=1)
        level = jnp.concatenate([piece] + [across(piece, "expert", 2 * d) for d in (1, 2, 3)], axis=0)
        own_tokens = lax.dynamic_slice_in_dim(tokens, core * half, half, axis=1)
        peer_tokens = swap_cores(lax.dynamic_slice_in_dim(tokens, (1 - core) * half, half, axis=1))
        arrived, level, peer_tokens = lax.optimization_barrier((arrived, level, peer_tokens))
        level_y = across(level, "expert", 1)
        level_x = across(level, "groups", 1)
    peer = swap_cores(arrived)
    *held, hidden = ffn_near(arrived, occupancy, gate_weight, up_weight, down_weight)
    ours, theirs = ffn_far(peer, occupancy, hidden, *held)
    if staged:
        ours, theirs, level_y, level_x = lax.optimization_barrier((ours, theirs, level_y, level_x))
    summed = add_halves(ours, swap_cores(theirs))
    returned = lax.all_to_all(
        summed.reshape(experts, CAP, model_width), "expert", split_axis=0, concat_axis=0, tiled=True
    )
    if staged:
        level_xy = across(level_y, "groups", 1)
        place = jnp.stack([at // 2, at % 2, group])
        mine, theirs = half_logits(
            place, own_tokens, peer_tokens, level, level_y, level_x, level_xy
        )
        parts = (mine, swap_cores(theirs))
    else:
        parts = (dot_rows(lax.all_gather(router_weight, "expert", axis=0, tiled=True), tokens),)
    weights, kl_terms = router_terms(
        ids, slots, env_mask[None, :], policy_logits.T, parts, width
    )
    mixed = dot_columns(weights, returned.reshape(width, model_width)).astype(jnp.bfloat16)
    return (mixed, kl_terms[0])


def solution(mesh):
    in_specs = (
        P(("groups", "expert", "tensor"), None),
        P("expert", None),
        P("expert", None, "tensor"),
        P("expert", None, "tensor"),
        P("expert", "tensor", None),
        P(("groups", "expert", "tensor"), None),
        P(("groups", "expert", "tensor"), None),
        P(("groups", "expert", "tensor"), None),
        P("expert", "groups"),
        P(("groups", "expert", "tensor")),
    )
    out_specs = (P(("groups", "expert", "tensor"), None), P(("groups", "expert", "tensor")))
    return jax.shard_map(
        per_device, mesh=mesh, in_specs=in_specs, out_specs=out_specs, check_vma=False
    )
```

```python
import functools

import jax
import jax.numpy as jnp
from jax import lax
from jax.experimental import pallas as pl
from jax.experimental.pallas import tpu as pltpu
from jax.sharding import PartitionSpec as P

CAP = 8
SWAP = [(0, 1), (1, 0)]
WHOLE = pl.BlockSpec(memory_space=pltpu.VMEM)
LEFT = pl.BlockSpec(memory_space=pltpu.HBM)


def swap_cores(value):
    return lax.ppermute(value, "tensor", SWAP)


def across(value, axis, distance):
    size = lax.axis_size(axis)
    return lax.ppermute(value, axis, [(s, s ^ distance) for s in range(size)])


def dot_rows(left, right):
    return lax.dot_general(
        left, right, (((1,), (1,)), ((), ())), preferred_element_type=jnp.float32
    )


def dot_columns(left, right):
    return lax.dot_general(
        left, right, (((0,), (0,)), ((), ())), preferred_element_type=jnp.float32
    )


def params(mib):
    return pltpu.CompilerParams(vmem_limit_bytes=mib << 20)


def cost(flops, nbytes):
    return pl.CostEstimate(flops=flops, bytes_accessed=nbytes, transcendentals=0)


def buffer_hits(ids, slots, width):
    choices, tokens = ids.shape
    valid = (ids < width // CAP) & (slots < CAP)
    place = jnp.where(valid, ids * CAP + slots, -1)
    rows = lax.broadcasted_iota(jnp.int32, (width, tokens), 0)
    hits = rows == place[0:1, :]
    for k in range(1, choices):
        hits = hits | (rows == place[k : k + 1, :])
    return hits


def load_kernel(*refs):
    sems = refs[-1]
    count = (len(refs) - 1) // 2
    copies = [
        pltpu.make_async_copy(refs[n], refs[count + n], sems.at[n]) for n in range(count)
    ]
    for copy in copies:
        copy.start()
    for copy in copies:
        copy.wait()


def load(*weights):
    there = [pltpu.with_memory_space_constraint(w, pltpu.HBM) for w in weights]
    return pl.pallas_call(
        load_kernel,
        out_shape=tuple(jax.ShapeDtypeStruct(w.shape, w.dtype) for w in weights),
        in_specs=[LEFT] * len(weights),
        out_specs=(WHOLE,) * len(weights),
        scratch_shapes=[pltpu.SemaphoreType.DMA((len(weights),))],
        compiler_params=params(16),
        cost_estimate=cost(0, sum(2 * w.size for w in weights)),
        name="load",
    )(*there)


def masked_hidden(g, u, occupancy, order, side):
    count = g.shape[0]
    sources = occupancy.shape[1]
    row = lax.broadcasted_iota(jnp.int32, (count, sources), 0)
    column = lax.broadcasted_iota(jnp.int32, (count, sources), 1)
    here = column == 2 * ((row // CAP) ^ order) + side
    used = jnp.sum(jnp.where(here, occupancy[...], 0), axis=1, keepdims=True)
    live = row[:, 0:1] % CAP < used
    return jnp.where(live, g / (1.0 + jnp.exp(-g)) * u, 0.0).astype(jnp.bfloat16)


def ffn_kernel(parts, relative, own, peer, occupancy, gate, up, down, out_own, out_peer):
    count = own.shape[0]
    wide = down.shape[2] // parts
    order = lax.axis_index("expert") if relative else 0
    core = lax.axis_index("tensor")
    rows = jnp.concatenate([own[...], peer[...]], axis=0)
    g = jnp.dot(rows, gate[0], preferred_element_type=jnp.float32)
    u = jnp.dot(rows, up[0], preferred_element_type=jnp.float32)
    hidden = jnp.concatenate(
        [
            masked_hidden(g[:count], u[:count], occupancy, order, core),
            masked_hidden(g[count:], u[count:], occupancy, order, 1 - core),
        ],
        axis=0,
    )
    for part in range(parts):
        at = slice(part * wide, (part + 1) * wide)
        value = jnp.dot(hidden, down[0, :, at], preferred_element_type=jnp.float32)
        value = value.astype(jnp.bfloat16)
        out_own[:, at] = value[:count]
        out_peer[:, at] = value[count:]


def ffn(relative, own, peer, occupancy, gate, up, down):
    half = jax.ShapeDtypeStruct(own.shape, own.dtype)
    count, model_width = own.shape
    hidden_width = gate.shape[2]
    parts = 4 if model_width % 512 == 0 else 1
    return pl.pallas_call(
        functools.partial(ffn_kernel, parts, relative),
        out_shape=(half, half),
        in_specs=[WHOLE] * 6,
        out_specs=(WHOLE, WHOLE),
        compiler_params=params(16),
        cost_estimate=cost(12 * count * model_width * hidden_width, 6 * model_width * hidden_width),
        name="ffn",
    )(own, peer, occupancy, gate, up, down)


def add_kernel(relative, ours, other, out):
    value = ours[...].astype(jnp.float32) + other[...].astype(jnp.float32)
    order = lax.axis_index("expert") if relative else 0
    for block in range(out.shape[0]):
        out[block ^ order] = value[block * CAP : (block + 1) * CAP].astype(out.dtype)


def add_halves(relative, ours, other):
    rows, model_width = ours.shape
    return pl.pallas_call(
        functools.partial(add_kernel, relative),
        out_shape=jax.ShapeDtypeStruct((rows // CAP, CAP, model_width), ours.dtype),
        in_specs=[WHOLE] * 2,
        out_specs=WHOLE,
        compiler_params=params(16),
        cost_estimate=cost(ours.size, 6 * ours.size),
        name="add_halves",
    )(ours, other)


def logits_kernel(own_tokens, peer_tokens, *refs):
    levels, (out_own, out_peer) = refs[:-2], refs[-2:]
    expert, group = lax.axis_index("expert"), lax.axis_index("groups")
    rows = jnp.concatenate([level[...] for level in levels], axis=0)
    for tokens, out in ((own_tokens, out_own), (peer_tokens, out_peer)):
        value = dot_rows(rows, tokens[...])
        for near in range(2):
            for d in range(8):
                block = near * 8 + d
                at = 2 * (expert ^ d) + (group ^ near)
                at = pl.ds(pl.multiple_of(at * 8, 8), 8)
                out[at, :] = value[block * 8 : (block + 1) * 8]


def half_logits(own_tokens, peer_tokens, *levels):
    rows = sum(level.shape[0] for level in levels)
    count, model_width = own_tokens.shape
    out = jax.ShapeDtypeStruct((rows, count), jnp.float32)
    return pl.pallas_call(
        logits_kernel,
        out_shape=(out, out),
        in_specs=[WHOLE] * 6,
        out_specs=(WHOLE, WHOLE),
        compiler_params=params(16),
        cost_estimate=cost(4 * rows * count * model_width, 2 * model_width * (rows + 2 * count)),
        name="half_logits",
    )(own_tokens, peer_tokens, *levels)


def log_sigmoid(value):
    return jnp.minimum(value, 0.0) - jnp.log1p(jnp.exp(-jnp.abs(value)))


def terms_kernel(count, ids, slots, mask, policy, *refs):
    weights, kl = refs[count : count + 2]
    parts = refs[:count] + refs[count + 2 :]
    if len(parts) == 1:
        logits = parts[0][...]
    else:
        mine, theirs, whole = parts
        core = lax.axis_index("tensor")
        for block in range(mine.shape[0] // 16):
            for part, side in ((mine, core), (theirs, 1 - core)):
                at = pl.multiple_of(block * 32 + side * 16, 16)
                whole[pl.ds(at, 16), :] = part[block * 16 : (block + 1) * 16]
        logits = whole[...]
    experts, tokens = logits.shape
    width = weights.shape[0]
    window = width // CAP
    scores = 1.0 / (1.0 + jnp.exp(-logits))
    names = lax.broadcasted_iota(jnp.int32, (experts, tokens), 0)
    choices = ids[...]
    chosen = jnp.zeros((experts, tokens), jnp.float32)
    for k in range(choices.shape[0]):
        chosen = chosen + jnp.where(names == choices[k : k + 1, :], scores, 0.0)
    total = jnp.sum(chosen, axis=0, keepdims=True)
    shares = (2.5 * scores[:window] / total).astype(jnp.bfloat16).astype(jnp.float32)
    spread = jnp.broadcast_to(shares[:, None, :], (window, CAP, tokens)).reshape(width, tokens)
    hits = buffer_hits(choices, slots[...], width)
    weights[...] = jnp.where(hits, spread, 0.0).astype(jnp.bfloat16)
    log_p = log_sigmoid(logits) - jnp.log(jnp.sum(scores, axis=0, keepdims=True))
    q = policy[...]
    policy_scores = 1.0 / (1.0 + jnp.exp(-q))
    log_q = log_sigmoid(q) - jnp.log(jnp.sum(policy_scores, axis=0, keepdims=True))
    keep = (1 - mask[...]).astype(jnp.float32)
    kl[...] = keep * jnp.sum(jnp.exp(log_q) * (log_q - log_p), axis=0, keepdims=True)


def router_terms(ids, slots, mask, policy, parts, width):
    experts, tokens = policy.shape
    whole = [pltpu.VMEM(policy.shape, jnp.float32)] if len(parts) > 1 else []
    return pl.pallas_call(
        functools.partial(terms_kernel, len(parts)),
        out_shape=(
            jax.ShapeDtypeStruct((width, tokens), jnp.bfloat16),
            jax.ShapeDtypeStruct((1, tokens), jnp.float32),
        ),
        in_specs=[WHOLE] * (4 + len(parts)),
        out_specs=(WHOLE, WHOLE),
        scratch_shapes=whole,
        compiler_params=params(16),
        cost_estimate=cost(30 * experts * tokens, 12 * experts * tokens),
        name="router_terms",
    )(ids, slots, mask, policy, *parts)


def per_device(
    tokens,
    router_weight,
    gate_weight,
    up_weight,
    down_weight,
    policy_logits,
    expert_ids,
    slots,
    occupancy,
    env_mask,
):
    experts = lax.axis_size("expert")
    groups = lax.axis_size("groups")
    core = lax.axis_index("tensor")
    model_width = tokens.shape[1]
    width = experts * CAP
    staged = experts == 8 and groups == 2 and router_weight.shape[0] == 32
    ids, slots = expert_ids.T, slots.T

    hits = buffer_hits(ids, slots, width)
    outgoing = jnp.dot(hits.astype(jnp.bfloat16), tokens, preferred_element_type=jnp.float32)
    outgoing = outgoing.astype(jnp.bfloat16).reshape(experts, CAP, model_width)
    if staged:
        at, group = lax.axis_index("expert"), lax.axis_index("groups")
        piece = lax.dynamic_slice_in_dim(router_weight, (2 * core + group) * 8, 8, axis=0)
        blocks, pieces = [lax.dynamic_index_in_dim(outgoing, at, 0, keepdims=False)], [piece]
        for d in range(1, 8):
            block = lax.dynamic_index_in_dim(outgoing, at ^ d, 0, keepdims=False)
            if d < 6:
                pair = across(jnp.concatenate([block, piece], axis=0), "expert", d)
                block = pair[:CAP]
                pieces.append(pair[CAP:])
            else:
                block = across(block, "expert", d)
            blocks.append(block)
        level_a = jnp.concatenate(pieces[:4], axis=0)
        level_b = jnp.concatenate(pieces[4:], axis=0)
        level_b = jnp.concatenate([level_b, across(level_b, "expert", 2)], axis=0)
        next_a = across(level_a, "groups", 1)
        weights = (gate_weight, up_weight, down_weight)
        blocks[4], *weights = lax.optimization_barrier((blocks[4], *weights))
        held = load(*weights)
        arrived = jnp.concatenate(blocks, axis=0)
        arrived, level_b, next_a, *held = lax.optimization_barrier((arrived, level_b, next_a, *held))
    else:
        arrived = lax.all_to_all(outgoing, "expert", split_axis=0, concat_axis=0, tiled=True)
        arrived = arrived.reshape(width, model_width)
        held = (gate_weight, up_weight, down_weight)
    ours, theirs = ffn(staged, arrived, swap_cores(arrived), occupancy, *held)
    summed = add_halves(staged, ours, swap_cores(theirs))
    returned = lax.all_to_all(summed, "expert", split_axis=0, concat_axis=0, tiled=True)
    if staged:
        next_b = across(level_b, "groups", 1)
        peer_tokens = swap_cores(tokens)
        mine, theirs = half_logits(tokens, peer_tokens, level_a, level_b, next_a, next_b)
        parts = (mine, swap_cores(theirs))
    else:
        parts = (dot_rows(lax.all_gather(router_weight, "expert", axis=0, tiled=True), tokens),)
    weights, kl_terms = router_terms(
        ids, slots, env_mask[None, :], policy_logits.T, parts, width
    )
    mixed = dot_columns(weights, returned.reshape(width, model_width)).astype(jnp.bfloat16)
    return (mixed, kl_terms[0])


def solution(mesh):
    in_specs = (
        P(("groups", "expert", "tensor"), None),
        P("expert", None),
        P("expert", None, "tensor"),
        P("expert", None, "tensor"),
        P("expert", "tensor", None),
        P(("groups", "expert", "tensor"), None),
        P(("groups", "expert", "tensor"), None),
        P(("groups", "expert", "tensor"), None),
        P("expert", "groups"),
        P(("groups", "expert", "tensor")),
    )
    out_specs = (P(("groups", "expert", "tensor"), None), P(("groups", "expert", "tensor")))
    return jax.shard_map(
        per_device, mesh=mesh, in_specs=in_specs, out_specs=out_specs, check_vma=False
    )
```

```python
import functools

import jax
import jax.numpy as jnp
from jax import lax
from jax.experimental import pallas as pl
from jax.experimental.pallas import tpu as pltpu
from jax.sharding import PartitionSpec as P

CAP = 8
SWAP = [(0, 1), (1, 0)]
WHOLE = pl.BlockSpec(memory_space=pltpu.VMEM)
LEFT = pl.BlockSpec(memory_space=pltpu.HBM)


def swap_cores(value):
    return lax.ppermute(value, "tensor", SWAP)


def across(value, axis, distance):
    size = lax.axis_size(axis)
    return lax.ppermute(value, axis, [(s, s ^ distance) for s in range(size)])


def dot_rows(left, right):
    return lax.dot_general(
        left, right, (((1,), (1,)), ((), ())), preferred_element_type=jnp.float32
    )


def dot_columns(left, right):
    return lax.dot_general(
        left, right, (((0,), (0,)), ((), ())), preferred_element_type=jnp.float32
    )


def params(mib):
    return pltpu.CompilerParams(vmem_limit_bytes=mib << 20)


def cost(flops, nbytes):
    return pl.CostEstimate(flops=flops, bytes_accessed=nbytes, transcendentals=0)


def buffer_hits(ids, slots, width):
    choices, tokens = ids.shape
    valid = (ids < width // CAP) & (slots < CAP)
    place = jnp.where(valid, ids * CAP + slots, -1)
    rows = lax.broadcasted_iota(jnp.int32, (width, tokens), 0)
    hits = rows == place[0:1, :]
    for k in range(1, choices):
        hits = hits | (rows == place[k : k + 1, :])
    return hits


def load_kernel(*refs):
    sems = refs[-1]
    count = (len(refs) - 1) // 2
    copies = [
        pltpu.make_async_copy(refs[n], refs[count + n], sems.at[n]) for n in range(count)
    ]
    for copy in copies:
        copy.start()
    for copy in copies:
        copy.wait()


def load(*weights):
    there = [pltpu.with_memory_space_constraint(w, pltpu.HBM) for w in weights]
    return pl.pallas_call(
        load_kernel,
        out_shape=tuple(jax.ShapeDtypeStruct(w.shape, w.dtype) for w in weights),
        in_specs=[LEFT] * len(weights),
        out_specs=(WHOLE,) * len(weights),
        scratch_shapes=[pltpu.SemaphoreType.DMA((len(weights),))],
        compiler_params=params(16),
        cost_estimate=cost(0, sum(2 * w.size for w in weights)),
        name="load",
    )(*there)


def masked_hidden(g, u, occupancy, order, side):
    count = g.shape[0]
    sources = occupancy.shape[1]
    row = lax.broadcasted_iota(jnp.int32, (count, sources), 0)
    column = lax.broadcasted_iota(jnp.int32, (count, sources), 1)
    here = column == 2 * ((row // CAP) ^ order) + side
    used = jnp.sum(jnp.where(here, occupancy[...], 0), axis=1, keepdims=True)
    live = row[:, 0:1] % CAP < used
    return jnp.where(live, g / (1.0 + jnp.exp(-g)) * u, 0.0).astype(jnp.bfloat16)


def ffn_kernel(parts, relative, own, peer, occupancy, gate, up, down, out_own, out_peer):
    count = own.shape[0]
    wide = down.shape[2] // parts
    order = lax.axis_index("expert") if relative else 0
    core = lax.axis_index("tensor")
    rows = jnp.concatenate([own[...], peer[...]], axis=0)
    g = jnp.dot(rows, gate[0], preferred_element_type=jnp.float32)
    u = jnp.dot(rows, up[0], preferred_element_type=jnp.float32)
    hidden = jnp.concatenate(
        [
            masked_hidden(g[:count], u[:count], occupancy, order, core),
            masked_hidden(g[count:], u[count:], occupancy, order, 1 - core),
        ],
        axis=0,
    )
    for part in range(parts):
        at = slice(part * wide, (part + 1) * wide)
        value = jnp.dot(hidden, down[0, :, at], preferred_element_type=jnp.float32)
        value = value.astype(jnp.bfloat16)
        out_own[:, at] = value[:count]
        out_peer[:, at] = value[count:]


def ffn(relative, own, peer, occupancy, gate, up, down):
    half = jax.ShapeDtypeStruct(own.shape, own.dtype)
    count, model_width = own.shape
    hidden_width = gate.shape[2]
    parts = 4 if model_width % 512 == 0 else 1
    return pl.pallas_call(
        functools.partial(ffn_kernel, parts, relative),
        out_shape=(half, half),
        in_specs=[WHOLE] * 6,
        out_specs=(WHOLE, WHOLE),
        compiler_params=params(16),
        cost_estimate=cost(12 * count * model_width * hidden_width, 6 * model_width * hidden_width),
        name="ffn",
    )(own, peer, occupancy, gate, up, down)


def add_kernel(relative, ours, other, out):
    value = ours[...].astype(jnp.float32) + other[...].astype(jnp.float32)
    order = lax.axis_index("expert") if relative else 0
    for block in range(out.shape[0]):
        out[block ^ order] = value[block * CAP : (block + 1) * CAP].astype(out.dtype)


def add_halves(relative, ours, other):
    rows, model_width = ours.shape
    return pl.pallas_call(
        functools.partial(add_kernel, relative),
        out_shape=jax.ShapeDtypeStruct((rows // CAP, CAP, model_width), ours.dtype),
        in_specs=[WHOLE] * 2,
        out_specs=WHOLE,
        compiler_params=params(16),
        cost_estimate=cost(ours.size, 6 * ours.size),
        name="add_halves",
    )(ours, other)


def logits_kernel(own_tokens, peer_tokens, *refs):
    levels, (out_own, out_peer) = refs[:-2], refs[-2:]
    expert, group = lax.axis_index("expert"), lax.axis_index("groups")
    rows = jnp.concatenate([level[...] for level in levels], axis=0)
    places = [(expert ^ d) * 16 for d in range(4)]
    for side in range(2):
        places += [(expert ^ d) * 16 + (group ^ side) * 8 for d in range(4, 8)]
    for tokens, out in ((own_tokens, out_own), (peer_tokens, out_peer)):
        value = dot_rows(rows, tokens[...])
        first = 0
        for n, place in enumerate(places):
            count = 16 if n < 4 else 8
            at = pl.ds(pl.multiple_of(place, 8), count)
            out[at, :] = value[first : first + count]
            first += count


def half_logits(own_tokens, peer_tokens, *levels):
    rows = sum(level.shape[0] for level in levels)
    count, model_width = own_tokens.shape
    out = jax.ShapeDtypeStruct((rows, count), jnp.float32)
    return pl.pallas_call(
        logits_kernel,
        out_shape=(out, out),
        in_specs=[WHOLE] * (2 + len(levels)),
        out_specs=(WHOLE, WHOLE),
        compiler_params=params(16),
        cost_estimate=cost(4 * rows * count * model_width, 2 * model_width * (rows + 2 * count)),
        name="half_logits",
    )(own_tokens, peer_tokens, *levels)


def log_sigmoid(value):
    return jnp.minimum(value, 0.0) - jnp.log1p(jnp.exp(-jnp.abs(value)))


def terms_kernel(count, ids, slots, mask, policy, *refs):
    weights, kl = refs[count : count + 2]
    parts = refs[:count] + refs[count + 2 :]
    if len(parts) == 1:
        logits = parts[0][...]
    else:
        mine, theirs, whole = parts
        core = lax.axis_index("tensor")
        for block in range(mine.shape[0] // 16):
            for part, side in ((mine, core), (theirs, 1 - core)):
                at = pl.multiple_of(block * 32 + side * 16, 16)
                whole[pl.ds(at, 16), :] = part[block * 16 : (block + 1) * 16]
        logits = whole[...]
    experts, tokens = logits.shape
    width = weights.shape[0]
    window = width // CAP
    scores = 1.0 / (1.0 + jnp.exp(-logits))
    names = lax.broadcasted_iota(jnp.int32, (experts, tokens), 0)
    choices = ids[...]
    chosen = jnp.zeros((experts, tokens), jnp.float32)
    for k in range(choices.shape[0]):
        chosen = chosen + jnp.where(names == choices[k : k + 1, :], scores, 0.0)
    total = jnp.sum(chosen, axis=0, keepdims=True)
    shares = (2.5 * scores[:window] / total).astype(jnp.bfloat16).astype(jnp.float32)
    spread = jnp.broadcast_to(shares[:, None, :], (window, CAP, tokens)).reshape(width, tokens)
    hits = buffer_hits(choices, slots[...], width)
    weights[...] = jnp.where(hits, spread, 0.0).astype(jnp.bfloat16)
    log_p = log_sigmoid(logits) - jnp.log(jnp.sum(scores, axis=0, keepdims=True))
    q = policy[...]
    policy_scores = 1.0 / (1.0 + jnp.exp(-q))
    log_q = log_sigmoid(q) - jnp.log(jnp.sum(policy_scores, axis=0, keepdims=True))
    keep = (1 - mask[...]).astype(jnp.float32)
    kl[...] = keep * jnp.sum(jnp.exp(log_q) * (log_q - log_p), axis=0, keepdims=True)


def router_terms(ids, slots, mask, policy, parts, width):
    experts, tokens = policy.shape
    whole = [pltpu.VMEM(policy.shape, jnp.float32)] if len(parts) > 1 else []
    return pl.pallas_call(
        functools.partial(terms_kernel, len(parts)),
        out_shape=(
            jax.ShapeDtypeStruct((width, tokens), jnp.bfloat16),
            jax.ShapeDtypeStruct((1, tokens), jnp.float32),
        ),
        in_specs=[WHOLE] * (4 + len(parts)),
        out_specs=(WHOLE, WHOLE),
        scratch_shapes=whole,
        compiler_params=params(16),
        cost_estimate=cost(30 * experts * tokens, 12 * experts * tokens),
        name="router_terms",
    )(ids, slots, mask, policy, *parts)


def per_device(
    tokens,
    router_weight,
    gate_weight,
    up_weight,
    down_weight,
    policy_logits,
    expert_ids,
    slots,
    occupancy,
    env_mask,
):
    experts = lax.axis_size("expert")
    groups = lax.axis_size("groups")
    core = lax.axis_index("tensor")
    model_width = tokens.shape[1]
    width = experts * CAP
    staged = experts == 8 and groups == 2 and router_weight.shape[0] == 32
    ids, slots = expert_ids.T, slots.T

    hits = buffer_hits(ids, slots, width)
    outgoing = jnp.dot(hits.astype(jnp.bfloat16), tokens, preferred_element_type=jnp.float32)
    outgoing = outgoing.astype(jnp.bfloat16).reshape(experts, CAP, model_width)
    if staged:
        at, group = lax.axis_index("expert"), lax.axis_index("groups")
        mine = lax.dynamic_slice_in_dim(router_weight, core * 16, 16, axis=0)
        piece = lax.dynamic_slice_in_dim(router_weight, core * 16 + group * 8, 8, axis=0)
        blocks, near = [lax.dynamic_index_in_dim(outgoing, at, 0, keepdims=False)], [mine]
        far = []
        for d in range(1, 8):
            block = lax.dynamic_index_in_dim(outgoing, at ^ d, 0, keepdims=False)
            if d < 6:
                along = mine if d < 4 else piece
                pair = across(jnp.concatenate([block, along], axis=0), "expert", d)
                block = pair[:CAP]
                (near if d < 4 else far).append(pair[CAP:])
            else:
                block = across(block, "expert", d)
            blocks.append(block)
        level_a = jnp.concatenate(near, axis=0)
        level_b = jnp.concatenate(far, axis=0)
        weights = (gate_weight, up_weight, down_weight)
        blocks[4], *weights = lax.optimization_barrier((blocks[4], *weights))
        held = load(*weights)
        level_b, *held = lax.optimization_barrier((level_b, *held))
        level_b = jnp.concatenate([level_b, across(level_b, "expert", 2)], axis=0)
        arrived = jnp.concatenate(blocks, axis=0)
        arrived, *held = lax.optimization_barrier((arrived, *held))
    else:
        arrived = lax.all_to_all(outgoing, "expert", split_axis=0, concat_axis=0, tiled=True)
        arrived = arrived.reshape(width, model_width)
        held = (gate_weight, up_weight, down_weight)
    ours, theirs = ffn(staged, arrived, swap_cores(arrived), occupancy, *held)
    if staged:
        ours, theirs, level_b = lax.optimization_barrier((ours, theirs, level_b))
    summed = add_halves(staged, ours, swap_cores(theirs))
    returned = lax.all_to_all(summed, "expert", split_axis=0, concat_axis=0, tiled=True)
    if staged:
        next_b = across(level_b, "groups", 1)
        peer_tokens = swap_cores(tokens)
        mine, theirs = half_logits(tokens, peer_tokens, level_a, level_b, next_b)
        parts = (mine, swap_cores(theirs))
    else:
        parts = (dot_rows(lax.all_gather(router_weight, "expert", axis=0, tiled=True), tokens),)
    weights, kl_terms = router_terms(
        ids, slots, env_mask[None, :], policy_logits.T, parts, width
    )
    mixed = dot_columns(weights, returned.reshape(width, model_width)).astype(jnp.bfloat16)
    return (mixed, kl_terms[0])


def solution(mesh):
    in_specs = (
        P(("groups", "expert", "tensor"), None),
        P("expert", None),
        P("expert", None, "tensor"),
        P("expert", None, "tensor"),
        P("expert", "tensor", None),
        P(("groups", "expert", "tensor"), None),
        P(("groups", "expert", "tensor"), None),
        P(("groups", "expert", "tensor"), None),
        P("expert", "groups"),
        P(("groups", "expert", "tensor")),
    )
    out_specs = (P(("groups", "expert", "tensor"), None), P(("groups", "expert", "tensor")))
    return jax.shard_map(
        per_device, mesh=mesh, in_specs=in_specs, out_specs=out_specs, check_vma=False
    )
```

```python
import functools

import jax
import jax.numpy as jnp
from jax import lax
from jax.experimental import pallas as pl
from jax.experimental.pallas import tpu as pltpu
from jax.sharding import PartitionSpec as P

CAP = 8
SWAP = [(0, 1), (1, 0)]
WHOLE = pl.BlockSpec(memory_space=pltpu.VMEM)
LEFT = pl.BlockSpec(memory_space=pltpu.HBM)


def swap_cores(value):
    return lax.ppermute(value, "tensor", SWAP)


def across(value, axis, distance):
    size = lax.axis_size(axis)
    return lax.ppermute(value, axis, [(s, s ^ distance) for s in range(size)])


def dot_rows(left, right):
    return lax.dot_general(
        left, right, (((1,), (1,)), ((), ())), preferred_element_type=jnp.float32
    )


def dot_columns(left, right):
    return lax.dot_general(
        left, right, (((0,), (0,)), ((), ())), preferred_element_type=jnp.float32
    )


def params(mib):
    return pltpu.CompilerParams(vmem_limit_bytes=mib << 20)


def cost(flops, nbytes):
    return pl.CostEstimate(flops=flops, bytes_accessed=nbytes, transcendentals=0)


def buffer_hits(ids, slots, width):
    choices, tokens = ids.shape
    valid = (ids < width // CAP) & (slots < CAP)
    place = jnp.where(valid, ids * CAP + slots, -1)
    rows = lax.broadcasted_iota(jnp.int32, (width, tokens), 0)
    hits = rows == place[0:1, :]
    for k in range(1, choices):
        hits = hits | (rows == place[k : k + 1, :])
    return hits


def load_kernel(*refs):
    sems = refs[-1]
    count = (len(refs) - 1) // 2
    copies = [
        pltpu.make_async_copy(refs[n], refs[count + n], sems.at[n]) for n in range(count)
    ]
    for copy in copies:
        copy.start()
    for copy in copies:
        copy.wait()


def load(*weights):
    there = [pltpu.with_memory_space_constraint(w, pltpu.HBM) for w in weights]
    return pl.pallas_call(
        load_kernel,
        out_shape=tuple(jax.ShapeDtypeStruct(w.shape, w.dtype) for w in weights),
        in_specs=[LEFT] * len(weights),
        out_specs=(WHOLE,) * len(weights),
        scratch_shapes=[pltpu.SemaphoreType.DMA((len(weights),))],
        compiler_params=params(16),
        cost_estimate=cost(0, sum(2 * w.size for w in weights)),
        name="load",
    )(*there)


def masked_hidden(g, u, occupancy, order, side):
    count = g.shape[0]
    sources = occupancy.shape[1]
    row = lax.broadcasted_iota(jnp.int32, (count, sources), 0)
    column = lax.broadcasted_iota(jnp.int32, (count, sources), 1)
    here = column == 2 * ((row // CAP) ^ order) + side
    used = jnp.sum(jnp.where(here, occupancy[...], 0), axis=1, keepdims=True)
    live = row[:, 0:1] % CAP < used
    return jnp.where(live, g / (1.0 + jnp.exp(-g)) * u, 0.0).astype(jnp.bfloat16)


def ffn_kernel(parts, relative, own, peer, occupancy, gate, up, down, out_own, out_peer):
    count = own.shape[0]
    wide = down.shape[2] // parts
    order = lax.axis_index("expert") if relative else 0
    core = lax.axis_index("tensor")
    rows = jnp.concatenate([own[...], peer[...]], axis=0)
    g = jnp.dot(rows, gate[0], preferred_element_type=jnp.float32)
    u = jnp.dot(rows, up[0], preferred_element_type=jnp.float32)
    hidden = jnp.concatenate(
        [
            masked_hidden(g[:count], u[:count], occupancy, order, core),
            masked_hidden(g[count:], u[count:], occupancy, order, 1 - core),
        ],
        axis=0,
    )
    for part in range(parts):
        at = slice(part * wide, (part + 1) * wide)
        value = jnp.dot(hidden, down[0, :, at], preferred_element_type=jnp.float32)
        value = value.astype(jnp.bfloat16)
        out_own[:, at] = value[:count]
        out_peer[:, at] = value[count:]


def ffn(relative, own, peer, occupancy, gate, up, down):
    half = jax.ShapeDtypeStruct(own.shape, own.dtype)
    count, model_width = own.shape
    hidden_width = gate.shape[2]
    parts = 4 if model_width % 512 == 0 else 1
    return pl.pallas_call(
        functools.partial(ffn_kernel, parts, relative),
        out_shape=(half, half),
        in_specs=[WHOLE] * 6,
        out_specs=(WHOLE, WHOLE),
        compiler_params=params(16),
        cost_estimate=cost(12 * count * model_width * hidden_width, 6 * model_width * hidden_width),
        name="ffn",
    )(own, peer, occupancy, gate, up, down)


def add_kernel(relative, ours, other, out):
    value = ours[...].astype(jnp.float32) + other[...].astype(jnp.float32)
    order = lax.axis_index("expert") if relative else 0
    for block in range(out.shape[0]):
        out[block ^ order] = value[block * CAP : (block + 1) * CAP].astype(out.dtype)


def add_halves(relative, ours, other):
    rows, model_width = ours.shape
    return pl.pallas_call(
        functools.partial(add_kernel, relative),
        out_shape=jax.ShapeDtypeStruct((rows // CAP, CAP, model_width), ours.dtype),
        in_specs=[WHOLE] * 2,
        out_specs=WHOLE,
        compiler_params=params(16),
        cost_estimate=cost(ours.size, 6 * ours.size),
        name="add_halves",
    )(ours, other)


def logits_kernel(own_tokens, peer_tokens, *refs):
    levels, (out_own, out_peer) = refs[:-2], refs[-2:]
    expert, group = lax.axis_index("expert"), lax.axis_index("groups")
    rows = jnp.concatenate([level[...] for level in levels], axis=0)
    places = [(expert ^ d) * 16 for d in range(4)]
    for side in range(2):
        places += [(expert ^ d) * 16 + (group ^ side) * 8 for d in range(4, 8)]
    for tokens, out in ((own_tokens, out_own), (peer_tokens, out_peer)):
        value = dot_rows(rows, tokens[...])
        first = 0
        for n, place in enumerate(places):
            count = 16 if n < 4 else 8
            at = pl.ds(pl.multiple_of(place, 8), count)
            out[at, :] = value[first : first + count]
            first += count


def half_logits(own_tokens, peer_tokens, *levels):
    rows = sum(level.shape[0] for level in levels)
    count, model_width = own_tokens.shape
    out = jax.ShapeDtypeStruct((rows, count), jnp.float32)
    return pl.pallas_call(
        logits_kernel,
        out_shape=(out, out),
        in_specs=[WHOLE] * (2 + len(levels)),
        out_specs=(WHOLE, WHOLE),
        compiler_params=params(16),
        cost_estimate=cost(4 * rows * count * model_width, 2 * model_width * (rows + 2 * count)),
        name="half_logits",
    )(own_tokens, peer_tokens, *levels)


def log_sigmoid(value):
    return jnp.minimum(value, 0.0) - jnp.log1p(jnp.exp(-jnp.abs(value)))


def terms_kernel(count, ids, slots, mask, policy, *refs):
    weights, kl = refs[count : count + 2]
    parts = refs[:count] + refs[count + 2 :]
    if len(parts) == 1:
        logits = parts[0][...]
    else:
        mine, theirs, whole = parts
        core = lax.axis_index("tensor")
        for block in range(mine.shape[0] // 16):
            for part, side in ((mine, core), (theirs, 1 - core)):
                at = pl.multiple_of(block * 32 + side * 16, 16)
                whole[pl.ds(at, 16), :] = part[block * 16 : (block + 1) * 16]
        logits = whole[...]
    experts, tokens = logits.shape
    width = weights.shape[0]
    window = width // CAP
    scores = 1.0 / (1.0 + jnp.exp(-logits))
    names = lax.broadcasted_iota(jnp.int32, (experts, tokens), 0)
    choices = ids[...]
    chosen = jnp.zeros((experts, tokens), jnp.float32)
    for k in range(choices.shape[0]):
        chosen = chosen + jnp.where(names == choices[k : k + 1, :], scores, 0.0)
    total = jnp.sum(chosen, axis=0, keepdims=True)
    shares = (2.5 * scores[:window] / total).astype(jnp.bfloat16).astype(jnp.float32)
    spread = jnp.broadcast_to(shares[:, None, :], (window, CAP, tokens)).reshape(width, tokens)
    hits = buffer_hits(choices, slots[...], width)
    weights[...] = jnp.where(hits, spread, 0.0).astype(jnp.bfloat16)
    log_p = log_sigmoid(logits) - jnp.log(jnp.sum(scores, axis=0, keepdims=True))
    q = policy[...]
    policy_scores = 1.0 / (1.0 + jnp.exp(-q))
    log_q = log_sigmoid(q) - jnp.log(jnp.sum(policy_scores, axis=0, keepdims=True))
    keep = (1 - mask[...]).astype(jnp.float32)
    kl[...] = keep * jnp.sum(jnp.exp(log_q) * (log_q - log_p), axis=0, keepdims=True)


def router_terms(ids, slots, mask, policy, parts, width):
    experts, tokens = policy.shape
    whole = [pltpu.VMEM(policy.shape, jnp.float32)] if len(parts) > 1 else []
    return pl.pallas_call(
        functools.partial(terms_kernel, len(parts)),
        out_shape=(
            jax.ShapeDtypeStruct((width, tokens), jnp.bfloat16),
            jax.ShapeDtypeStruct((1, tokens), jnp.float32),
        ),
        in_specs=[WHOLE] * (4 + len(parts)),
        out_specs=(WHOLE, WHOLE),
        scratch_shapes=whole,
        compiler_params=params(16),
        cost_estimate=cost(30 * experts * tokens, 12 * experts * tokens),
        name="router_terms",
    )(ids, slots, mask, policy, *parts)


def per_device(
    tokens,
    router_weight,
    gate_weight,
    up_weight,
    down_weight,
    policy_logits,
    expert_ids,
    slots,
    occupancy,
    env_mask,
):
    experts = lax.axis_size("expert")
    groups = lax.axis_size("groups")
    core = lax.axis_index("tensor")
    model_width = tokens.shape[1]
    width = experts * CAP
    staged = experts == 8 and groups == 2 and router_weight.shape[0] == 32
    ids, slots = expert_ids.T, slots.T

    hits = buffer_hits(ids, slots, width)
    outgoing = jnp.dot(hits.astype(jnp.bfloat16), tokens, preferred_element_type=jnp.float32)
    outgoing = outgoing.astype(jnp.bfloat16).reshape(experts, CAP, model_width)
    if staged:
        at, group = lax.axis_index("expert"), lax.axis_index("groups")
        mine = lax.dynamic_slice_in_dim(router_weight, core * 16, 16, axis=0)
        piece = lax.dynamic_slice_in_dim(router_weight, core * 16 + group * 8, 8, axis=0)
        blocks = {0: lax.dynamic_index_in_dim(outgoing, at, 0, keepdims=False)}
        send = {}
        for d in range(1, 8):
            block = lax.dynamic_index_in_dim(outgoing, at ^ d, 0, keepdims=False)
            along = [mine] if d < 4 else [piece] if d < 6 else []
            send[d] = jnp.concatenate([block] + along, axis=0)
        for d, before in ((4, 0), (2, 0), (3, 0), (5, 0), (6, 0), (7, 4), (1, 2)):
            if before:
                blocks[before], send[d] = lax.optimization_barrier((blocks[before], send[d]))
            blocks[d] = across(send[d], "expert", d)
        level_a = jnp.concatenate([mine] + [blocks[d][CAP:] for d in (1, 2, 3)], axis=0)
        weights = (gate_weight, up_weight, down_weight)
        blocks[4], *weights = lax.optimization_barrier((blocks[4], *weights))
        held = load(*weights)
        level_b = jnp.concatenate([blocks[d][CAP:] for d in (4, 5)], axis=0)
        level_b, *held = lax.optimization_barrier((level_b, *held))
        level_b = jnp.concatenate([level_b, across(level_b, "expert", 2)], axis=0)
        arrived = jnp.concatenate([blocks[d][:CAP] for d in range(8)], axis=0)
        arrived, *held = lax.optimization_barrier((arrived, *held))
    else:
        arrived = lax.all_to_all(outgoing, "expert", split_axis=0, concat_axis=0, tiled=True)
        arrived = arrived.reshape(width, model_width)
        held = (gate_weight, up_weight, down_weight)
    ours, theirs = ffn(staged, arrived, swap_cores(arrived), occupancy, *held)
    other = swap_cores(theirs)
    if staged:
        other, level_b = lax.optimization_barrier((other, level_b))
    summed = add_halves(staged, ours, other)
    returned = lax.all_to_all(summed, "expert", split_axis=0, concat_axis=0, tiled=True)
    if staged:
        next_b = across(level_b, "groups", 1)
        peer_tokens = swap_cores(tokens)
        mine, theirs = half_logits(tokens, peer_tokens, level_a, level_b, next_b)
        parts = (mine, swap_cores(theirs))
    else:
        parts = (dot_rows(lax.all_gather(router_weight, "expert", axis=0, tiled=True), tokens),)
    weights, kl_terms = router_terms(
        ids, slots, env_mask[None, :], policy_logits.T, parts, width
    )
    mixed = dot_columns(weights, returned.reshape(width, model_width)).astype(jnp.bfloat16)
    return (mixed, kl_terms[0])


def solution(mesh):
    in_specs = (
        P(("groups", "expert", "tensor"), None),
        P("expert", None),
        P("expert", None, "tensor"),
        P("expert", None, "tensor"),
        P("expert", "tensor", None),
        P(("groups", "expert", "tensor"), None),
        P(("groups", "expert", "tensor"), None),
        P(("groups", "expert", "tensor"), None),
        P("expert", "groups"),
        P(("groups", "expert", "tensor")),
    )
    out_specs = (P(("groups", "expert", "tensor"), None), P(("groups", "expert", "tensor")))
    return jax.shard_map(
        per_device, mesh=mesh, in_specs=in_specs, out_specs=out_specs, check_vma=False
    )
```

```python
import functools

import jax
import jax.numpy as jnp
from jax import lax
from jax.experimental import pallas as pl
from jax.experimental.pallas import tpu as pltpu
from jax.sharding import PartitionSpec as P

CAP = 8
SWAP = [(0, 1), (1, 0)]
WHOLE = pl.BlockSpec(memory_space=pltpu.VMEM)
LEFT = pl.BlockSpec(memory_space=pltpu.HBM)


def swap_cores(value):
    return lax.ppermute(value, "tensor", SWAP)


def across(value, axis, distance):
    size = lax.axis_size(axis)
    return lax.ppermute(value, axis, [(s, s ^ distance) for s in range(size)])


def dot_rows(left, right):
    return lax.dot_general(
        left, right, (((1,), (1,)), ((), ())), preferred_element_type=jnp.float32
    )


def params(mib):
    return pltpu.CompilerParams(vmem_limit_bytes=mib << 20)


def cost(flops, nbytes):
    return pl.CostEstimate(flops=flops, bytes_accessed=nbytes, transcendentals=0)


def buffer_hits(ids, slots, width):
    choices, tokens = ids.shape
    valid = (ids < width // CAP) & (slots < CAP)
    place = jnp.where(valid, ids * CAP + slots, -1)
    rows = lax.broadcasted_iota(jnp.int32, (width, tokens), 0)
    hits = rows == place[0:1, :]
    for k in range(1, choices):
        hits = hits | (rows == place[k : k + 1, :])
    return hits


def load_kernel(*refs):
    sems = refs[-1]
    count = (len(refs) - 1) // 2
    copies = [
        pltpu.make_async_copy(refs[n], refs[count + n], sems.at[n]) for n in range(count)
    ]
    for copy in copies:
        copy.start()
    for copy in copies:
        copy.wait()


def load(*weights):
    there = [pltpu.with_memory_space_constraint(w, pltpu.HBM) for w in weights]
    return pl.pallas_call(
        load_kernel,
        out_shape=tuple(jax.ShapeDtypeStruct(w.shape, w.dtype) for w in weights),
        in_specs=[LEFT] * len(weights),
        out_specs=(WHOLE,) * len(weights),
        scratch_shapes=[pltpu.SemaphoreType.DMA((len(weights),))],
        compiler_params=params(16),
        cost_estimate=cost(0, sum(2 * w.size for w in weights)),
        name="load",
    )(*there)


def masked_hidden(g, u, occupancy, order, side):
    count = g.shape[0]
    sources = occupancy.shape[1]
    row = lax.broadcasted_iota(jnp.int32, (count, sources), 0)
    column = lax.broadcasted_iota(jnp.int32, (count, sources), 1)
    here = column == 2 * ((row // CAP) ^ order) + side
    used = jnp.sum(jnp.where(here, occupancy[...], 0), axis=1, keepdims=True)
    live = row[:, 0:1] % CAP < used
    return jnp.where(live, g / (1.0 + jnp.exp(-g)) * u, 0.0).astype(jnp.bfloat16)


def ffn_kernel(parts, relative, own, peer, occupancy, gate, up, down, out_own, out_peer):
    count = own.shape[0]
    wide = down.shape[2] // parts
    order = lax.axis_index("expert") if relative else 0
    core = lax.axis_index("tensor")
    rows = jnp.concatenate([own[...], peer[...]], axis=0)
    g = jnp.dot(rows, gate[0], preferred_element_type=jnp.float32)
    u = jnp.dot(rows, up[0], preferred_element_type=jnp.float32)
    hidden = jnp.concatenate(
        [
            masked_hidden(g[:count], u[:count], occupancy, order, core),
            masked_hidden(g[count:], u[count:], occupancy, order, 1 - core),
        ],
        axis=0,
    )
    for part in range(parts):
        at = slice(part * wide, (part + 1) * wide)
        value = jnp.dot(hidden, down[0, :, at], preferred_element_type=jnp.float32)
        value = value.astype(jnp.bfloat16)
        out_own[:, at] = value[:count]
        out_peer[:, at] = value[count:]


def ffn(relative, own, peer, occupancy, gate, up, down):
    half = jax.ShapeDtypeStruct(own.shape, own.dtype)
    count, model_width = own.shape
    hidden_width = gate.shape[2]
    parts = 4 if model_width % 512 == 0 else 1
    return pl.pallas_call(
        functools.partial(ffn_kernel, parts, relative),
        out_shape=(half, half),
        in_specs=[WHOLE] * 6,
        out_specs=(WHOLE, WHOLE),
        compiler_params=params(16),
        cost_estimate=cost(12 * count * model_width * hidden_width, 6 * model_width * hidden_width),
        name="ffn",
    )(own, peer, occupancy, gate, up, down)


def add_kernel(relative, ours, other, out, here, sems):
    value = ours[...].astype(jnp.float32) + other[...].astype(jnp.float32)
    order = lax.axis_index("expert") if relative else 0
    copies = []
    for block in range(out.shape[0]):
        here[block] = value[block * CAP : (block + 1) * CAP].astype(here.dtype)
        copies.append(
            pltpu.make_async_copy(here.at[block], out.at[block ^ order], sems.at[block])
        )
        copies[block].start()
    for copy in copies:
        copy.wait()


def add_halves(relative, ours, other):
    rows, model_width = ours.shape
    shape = (rows // CAP, CAP, model_width)
    return pl.pallas_call(
        functools.partial(add_kernel, relative),
        out_shape=jax.ShapeDtypeStruct(shape, ours.dtype),
        in_specs=[WHOLE] * 2,
        out_specs=LEFT,
        scratch_shapes=[
            pltpu.VMEM(shape, ours.dtype),
            pltpu.SemaphoreType.DMA((rows // CAP,)),
        ],
        compiler_params=params(16),
        cost_estimate=cost(ours.size, 6 * ours.size),
        name="add_halves",
    )(ours, other)


def logits_kernel(own_tokens, peer_tokens, *refs):
    levels, (out_own, out_peer) = refs[:-2], refs[-2:]
    expert, group = lax.axis_index("expert"), lax.axis_index("groups")
    rows = jnp.concatenate([level[...] for level in levels], axis=0)
    places = [(expert ^ d) * 16 for d in (0, 2, 3)]
    for side in range(2):
        places += [(expert ^ d) * 16 + (group ^ side) * 8 for d in (1, 4, 5, 6, 7)]
    for tokens, out in ((own_tokens, out_own), (peer_tokens, out_peer)):
        value = dot_rows(rows, tokens[...])
        first = 0
        for n, place in enumerate(places):
            count = 16 if n < 3 else 8
            at = pl.ds(pl.multiple_of(place, 8), count)
            out[at, :] = value[first : first + count]
            first += count


def half_logits(own_tokens, peer_tokens, *levels):
    rows = sum(level.shape[0] for level in levels)
    count, model_width = own_tokens.shape
    out = jax.ShapeDtypeStruct((rows, count), jnp.float32)
    return pl.pallas_call(
        logits_kernel,
        out_shape=(out, out),
        in_specs=[WHOLE] * (2 + len(levels)),
        out_specs=(WHOLE, WHOLE),
        compiler_params=params(16),
        cost_estimate=cost(4 * rows * count * model_width, 2 * model_width * (rows + 2 * count)),
        name="half_logits",
    )(own_tokens, peer_tokens, *levels)


def log_sigmoid(value):
    return jnp.minimum(value, 0.0) - jnp.log1p(jnp.exp(-jnp.abs(value)))


def terms_kernel(count, ids, slots, mask, policy, *refs):
    weights, kl = refs[count : count + 2]
    parts = refs[:count] + refs[count + 2 :]
    if len(parts) == 1:
        logits = parts[0][...]
    else:
        mine, theirs, whole = parts
        core = lax.axis_index("tensor")
        for block in range(mine.shape[0] // 16):
            for part, side in ((mine, core), (theirs, 1 - core)):
                at = pl.multiple_of(block * 32 + side * 16, 16)
                whole[pl.ds(at, 16), :] = part[block * 16 : (block + 1) * 16]
        logits = whole[...]
    experts, tokens = logits.shape
    width = weights.shape[1]
    window = width // CAP
    scores = 1.0 / (1.0 + jnp.exp(-logits))
    names = lax.broadcasted_iota(jnp.int32, (experts, tokens), 0)
    choices = ids[...]
    chosen = jnp.zeros((experts, tokens), jnp.float32)
    for k in range(choices.shape[0]):
        chosen = chosen + jnp.where(names == choices[k : k + 1, :], scores, 0.0)
    total = jnp.sum(chosen, axis=0, keepdims=True)
    shares = (2.5 * scores[:window] / total).astype(jnp.bfloat16).astype(jnp.float32)
    spread = jnp.broadcast_to(shares[:, None, :], (window, CAP, tokens)).reshape(width, tokens)
    hits = buffer_hits(choices, slots[...], width)
    weights[...] = jnp.where(hits, spread, 0.0).T.astype(jnp.bfloat16)
    log_p = log_sigmoid(logits) - jnp.log(jnp.sum(scores, axis=0, keepdims=True))
    q = policy[...]
    policy_scores = 1.0 / (1.0 + jnp.exp(-q))
    log_q = log_sigmoid(q) - jnp.log(jnp.sum(policy_scores, axis=0, keepdims=True))
    keep = (1 - mask[...]).astype(jnp.float32)
    kl[...] = keep * jnp.sum(jnp.exp(log_q) * (log_q - log_p), axis=0, keepdims=True)


def router_terms(ids, slots, mask, policy, parts, width):
    experts, tokens = policy.shape
    whole = [pltpu.VMEM(policy.shape, jnp.float32)] if len(parts) > 1 else []
    return pl.pallas_call(
        functools.partial(terms_kernel, len(parts)),
        out_shape=(
            jax.ShapeDtypeStruct((tokens, width), jnp.bfloat16),
            jax.ShapeDtypeStruct((1, tokens), jnp.float32),
        ),
        in_specs=[WHOLE] * (4 + len(parts)),
        out_specs=(WHOLE, WHOLE),
        scratch_shapes=whole,
        compiler_params=params(16),
        cost_estimate=cost(30 * experts * tokens, 12 * experts * tokens),
        name="router_terms",
    )(ids, slots, mask, policy, *parts)


def combine_kernel(parts, weights, returned, out, here, sems):
    wide = returned.shape[1] // parts
    copies = []
    for part in range(parts):
        at = pl.ds(part * wide, wide)
        value = jnp.dot(weights[...], returned[:, at], preferred_element_type=jnp.float32)
        here[:, at] = value.astype(here.dtype)
        copies.append(pltpu.make_async_copy(here.at[:, at], out.at[:, at], sems.at[part]))
        copies[part].start()
    for copy in copies:
        copy.wait()


def combine(weights, returned):
    tokens, width = weights.shape
    model_width = returned.shape[1]
    parts = 4 if model_width % 512 == 0 else 1
    return pl.pallas_call(
        functools.partial(combine_kernel, parts),
        out_shape=jax.ShapeDtypeStruct((tokens, model_width), returned.dtype),
        in_specs=[WHOLE] * 2,
        out_specs=LEFT,
        scratch_shapes=[
            pltpu.VMEM((tokens, model_width), returned.dtype),
            pltpu.SemaphoreType.DMA((parts,)),
        ],
        compiler_params=params(16),
        cost_estimate=cost(2 * tokens * width * model_width, 2 * tokens * model_width),
        name="combine",
    )(weights, returned)


def per_device(
    tokens,
    router_weight,
    gate_weight,
    up_weight,
    down_weight,
    policy_logits,
    expert_ids,
    slots,
    occupancy,
    env_mask,
):
    experts = lax.axis_size("expert")
    groups = lax.axis_size("groups")
    core = lax.axis_index("tensor")
    model_width = tokens.shape[1]
    width = experts * CAP
    staged = experts == 8 and groups == 2 and router_weight.shape[0] == 32
    ids, slots = expert_ids.T, slots.T

    hits = buffer_hits(ids, slots, width)
    outgoing = jnp.dot(hits.astype(jnp.bfloat16), tokens, preferred_element_type=jnp.float32)
    outgoing = outgoing.astype(jnp.bfloat16).reshape(experts, CAP, model_width)
    if staged:
        at, group = lax.axis_index("expert"), lax.axis_index("groups")
        mine = lax.dynamic_slice_in_dim(router_weight, core * 16, 16, axis=0)
        piece = lax.dynamic_slice_in_dim(router_weight, core * 16 + group * 8, 8, axis=0)
        blocks = {0: lax.dynamic_index_in_dim(outgoing, at, 0, keepdims=False)}
        send = {}
        for d in range(1, 8):
            block = lax.dynamic_index_in_dim(outgoing, at ^ d, 0, keepdims=False)
            along = [mine] if d in (2, 3) else [piece] if d < 5 else []
            send[d] = jnp.concatenate([block] + along, axis=0)
        for d, before in ((4, 0), (2, 0), (3, 0), (6, 0), (7, 0), (5, 4), (1, 2)):
            if before:
                blocks[before], send[d] = lax.optimization_barrier((blocks[before], send[d]))
            if d == 1:
                send[d] = jnp.concatenate([send[d], blocks[4][CAP:]], axis=0)
            blocks[d] = across(send[d], "expert", d)
        level_a = jnp.concatenate([mine] + [blocks[d][CAP : CAP + 16] for d in (2, 3)], axis=0)
        weights = (gate_weight, up_weight, down_weight)
        blocks[4], *weights = lax.optimization_barrier((blocks[4], *weights))
        held = load(*weights)
        level_b = jnp.concatenate([blocks[4][CAP:], blocks[1][2 * CAP :]], axis=0)
        level_b, *held = lax.optimization_barrier((level_b, *held))
        level_b = jnp.concatenate(
            [blocks[1][CAP : 2 * CAP], level_b, across(level_b, "expert", 2)], axis=0
        )
        arrived = jnp.concatenate([blocks[d][:CAP] for d in range(8)], axis=0)
        arrived, *held = lax.optimization_barrier((arrived, *held))
    else:
        arrived = lax.all_to_all(outgoing, "expert", split_axis=0, concat_axis=0, tiled=True)
        arrived = arrived.reshape(width, model_width)
        held = (gate_weight, up_weight, down_weight)
    ours, theirs = ffn(staged, arrived, swap_cores(arrived), occupancy, *held)
    other = swap_cores(theirs)
    if staged:
        other, level_b = lax.optimization_barrier((other, level_b))
    summed = add_halves(staged, ours, other)
    returned = lax.all_to_all(summed, "expert", split_axis=0, concat_axis=0, tiled=True)
    if staged:
        next_b = across(level_b, "groups", 1)
        peer_tokens = swap_cores(tokens)
        mine, theirs = half_logits(tokens, peer_tokens, level_a, level_b, next_b)
        parts = (mine, swap_cores(theirs))
    else:
        parts = (dot_rows(lax.all_gather(router_weight, "expert", axis=0, tiled=True), tokens),)
    weights, kl_terms = router_terms(
        ids, slots, env_mask[None, :], policy_logits.T, parts, width
    )
    return (combine(weights, returned.reshape(width, model_width)), kl_terms[0])


def solution(mesh):
    in_specs = (
        P(("groups", "expert", "tensor"), None),
        P("expert", None),
        P("expert", None, "tensor"),
        P("expert", None, "tensor"),
        P("expert", "tensor", None),
        P(("groups", "expert", "tensor"), None),
        P(("groups", "expert", "tensor"), None),
        P(("groups", "expert", "tensor"), None),
        P("expert", "groups"),
        P(("groups", "expert", "tensor")),
    )
    out_specs = (P(("groups", "expert", "tensor"), None), P(("groups", "expert", "tensor")))
    return jax.shard_map(
        per_device, mesh=mesh, in_specs=in_specs, out_specs=out_specs, check_vma=False
    )
```

```python
import functools

import jax
import jax.numpy as jnp
from jax import lax
from jax.experimental import pallas as pl
from jax.experimental.pallas import tpu as pltpu
from jax.sharding import PartitionSpec as P

CAP = 8
SWAP = [(0, 1), (1, 0)]
WHOLE = pl.BlockSpec(memory_space=pltpu.VMEM)
LEFT = pl.BlockSpec(memory_space=pltpu.HBM)


def swap_cores(value):
    return lax.ppermute(value, "tensor", SWAP)


def across(value, axis, distance):
    size = lax.axis_size(axis)
    return lax.ppermute(value, axis, [(s, s ^ distance) for s in range(size)])


def dot_rows(left, right):
    return lax.dot_general(
        left, right, (((1,), (1,)), ((), ())), preferred_element_type=jnp.float32
    )


def params(mib):
    return pltpu.CompilerParams(vmem_limit_bytes=mib << 20)


def cost(flops, nbytes):
    return pl.CostEstimate(flops=flops, bytes_accessed=nbytes, transcendentals=0)


def buffer_hits(ids, slots, width):
    choices, tokens = ids.shape
    valid = (ids < width // CAP) & (slots < CAP)
    place = jnp.where(valid, ids * CAP + slots, -1)
    rows = lax.broadcasted_iota(jnp.int32, (width, tokens), 0)
    hits = rows == place[0:1, :]
    for k in range(1, choices):
        hits = hits | (rows == place[k : k + 1, :])
    return hits


def load_kernel(*refs):
    sems = refs[-1]
    count = (len(refs) - 1) // 2
    copies = [
        pltpu.make_async_copy(refs[n], refs[count + n], sems.at[n]) for n in range(count)
    ]
    for copy in copies:
        copy.start()
    for copy in copies:
        copy.wait()


def load(*weights):
    there = [pltpu.with_memory_space_constraint(w, pltpu.HBM) for w in weights]
    return pl.pallas_call(
        load_kernel,
        out_shape=tuple(jax.ShapeDtypeStruct(w.shape, w.dtype) for w in weights),
        in_specs=[LEFT] * len(weights),
        out_specs=(WHOLE,) * len(weights),
        scratch_shapes=[pltpu.SemaphoreType.DMA((len(weights),))],
        compiler_params=params(16),
        cost_estimate=cost(0, sum(2 * w.size for w in weights)),
        name="load",
    )(*there)


def masked_hidden(g, u, occupancy, order, side):
    count = g.shape[0]
    sources = occupancy.shape[1]
    row = lax.broadcasted_iota(jnp.int32, (count, sources), 0)
    column = lax.broadcasted_iota(jnp.int32, (count, sources), 1)
    here = column == 2 * ((row // CAP) ^ order) + side
    used = jnp.sum(jnp.where(here, occupancy[...], 0), axis=1, keepdims=True)
    live = row[:, 0:1] % CAP < used
    return jnp.where(live, g / (1.0 + jnp.exp(-g)) * u, 0.0).astype(jnp.bfloat16)


def ffn_kernel(parts, relative, own, peer, occupancy, gate, up, down, out_own, out_peer):
    count = own.shape[0]
    wide = down.shape[2] // parts
    order = lax.axis_index("expert") if relative else 0
    core = lax.axis_index("tensor")
    rows = jnp.concatenate([own[...], peer[...]], axis=0)
    g = jnp.dot(rows, gate[0], preferred_element_type=jnp.float32)
    u = jnp.dot(rows, up[0], preferred_element_type=jnp.float32)
    hidden = jnp.concatenate(
        [
            masked_hidden(g[:count], u[:count], occupancy, order, core),
            masked_hidden(g[count:], u[count:], occupancy, order, 1 - core),
        ],
        axis=0,
    )
    for part in range(parts):
        at = slice(part * wide, (part + 1) * wide)
        value = jnp.dot(hidden, down[0, :, at], preferred_element_type=jnp.float32)
        value = value.astype(jnp.bfloat16)
        out_own[:, at] = value[:count]
        out_peer[:, at] = value[count:]


def ffn(relative, own, peer, occupancy, gate, up, down):
    half = jax.ShapeDtypeStruct(own.shape, own.dtype)
    count, model_width = own.shape
    hidden_width = gate.shape[2]
    parts = 4 if model_width % 512 == 0 else 1
    return pl.pallas_call(
        functools.partial(ffn_kernel, parts, relative),
        out_shape=(half, half),
        in_specs=[WHOLE] * 6,
        out_specs=(WHOLE, WHOLE),
        compiler_params=params(16),
        cost_estimate=cost(12 * count * model_width * hidden_width, 6 * model_width * hidden_width),
        name="ffn",
    )(own, peer, occupancy, gate, up, down)


def add_kernel(relative, ours, other, out, here, sems):
    value = ours[...].astype(jnp.float32) + other[...].astype(jnp.float32)
    order = lax.axis_index("expert") if relative else 0
    copies = []
    for block in range(out.shape[0]):
        here[block] = value[block * CAP : (block + 1) * CAP].astype(here.dtype)
        copies.append(
            pltpu.make_async_copy(here.at[block], out.at[block ^ order], sems.at[block])
        )
        copies[block].start()
    for copy in copies:
        copy.wait()


def add_halves(relative, ours, other):
    rows, model_width = ours.shape
    shape = (rows // CAP, CAP, model_width)
    return pl.pallas_call(
        functools.partial(add_kernel, relative),
        out_shape=jax.ShapeDtypeStruct(shape, ours.dtype),
        in_specs=[WHOLE] * 2,
        out_specs=LEFT,
        scratch_shapes=[
            pltpu.VMEM(shape, ours.dtype),
            pltpu.SemaphoreType.DMA((rows // CAP,)),
        ],
        compiler_params=params(16),
        cost_estimate=cost(ours.size, 6 * ours.size),
        name="add_halves",
    )(ours, other)


def logits_kernel(own_tokens, peer_tokens, *refs):
    levels, (out_own, out_peer) = refs[:-2], refs[-2:]
    expert, group = lax.axis_index("expert"), lax.axis_index("groups")
    rows = jnp.concatenate([level[...] for level in levels], axis=0)
    places = [(expert ^ d) * 16 for d in (0, 2, 3)]
    for side in range(2):
        places += [(expert ^ d) * 16 + (group ^ side) * 8 for d in (1, 4, 5, 6, 7)]
    for tokens, out in ((own_tokens, out_own), (peer_tokens, out_peer)):
        value = dot_rows(rows, tokens[...])
        first = 0
        for n, place in enumerate(places):
            count = 16 if n < 3 else 8
            at = pl.ds(pl.multiple_of(place, 8), count)
            out[at, :] = value[first : first + count]
            first += count


def half_logits(own_tokens, peer_tokens, *levels):
    rows = sum(level.shape[0] for level in levels)
    count, model_width = own_tokens.shape
    out = jax.ShapeDtypeStruct((rows, count), jnp.float32)
    return pl.pallas_call(
        logits_kernel,
        out_shape=(out, out),
        in_specs=[WHOLE] * (2 + len(levels)),
        out_specs=(WHOLE, WHOLE),
        compiler_params=params(16),
        cost_estimate=cost(4 * rows * count * model_width, 2 * model_width * (rows + 2 * count)),
        name="half_logits",
    )(own_tokens, peer_tokens, *levels)


def log_sigmoid(value):
    return jnp.minimum(value, 0.0) - jnp.log1p(jnp.exp(-jnp.abs(value)))


def terms_kernel(count, ids, slots, mask, policy, *refs):
    weights, kl = refs[count : count + 2]
    parts = refs[:count] + refs[count + 2 :]
    if len(parts) == 1:
        logits = parts[0][...]
    else:
        mine, theirs, whole = parts
        core = lax.axis_index("tensor")
        for block in range(mine.shape[0] // 16):
            for part, side in ((mine, core), (theirs, 1 - core)):
                at = pl.multiple_of(block * 32 + side * 16, 16)
                whole[pl.ds(at, 16), :] = part[block * 16 : (block + 1) * 16]
        logits = whole[...]
    experts, tokens = logits.shape
    width = weights.shape[1]
    window = width // CAP
    scores = 1.0 / (1.0 + jnp.exp(-logits))
    names = lax.broadcasted_iota(jnp.int32, (experts, tokens), 0)
    choices = ids[...]
    chosen = jnp.zeros((experts, tokens), jnp.float32)
    for k in range(choices.shape[0]):
        chosen = chosen + jnp.where(names == choices[k : k + 1, :], scores, 0.0)
    total = jnp.sum(chosen, axis=0, keepdims=True)
    shares = (2.5 * scores[:window] / total).astype(jnp.bfloat16).astype(jnp.float32)
    spread = jnp.broadcast_to(shares[:, None, :], (window, CAP, tokens)).reshape(width, tokens)
    hits = buffer_hits(choices, slots[...], width)
    weights[...] = jnp.where(hits, spread, 0.0).T.astype(jnp.bfloat16)
    log_p = log_sigmoid(logits) - jnp.log(jnp.sum(scores, axis=0, keepdims=True))
    q = policy[...]
    policy_scores = 1.0 / (1.0 + jnp.exp(-q))
    log_q = log_sigmoid(q) - jnp.log(jnp.sum(policy_scores, axis=0, keepdims=True))
    keep = (1 - mask[...]).astype(jnp.float32)
    kl[...] = keep * jnp.sum(jnp.exp(log_q) * (log_q - log_p), axis=0, keepdims=True)


def router_terms(ids, slots, mask, policy, parts, width):
    experts, tokens = policy.shape
    whole = [pltpu.VMEM(policy.shape, jnp.float32)] if len(parts) > 1 else []
    return pl.pallas_call(
        functools.partial(terms_kernel, len(parts)),
        out_shape=(
            jax.ShapeDtypeStruct((tokens, width), jnp.bfloat16),
            jax.ShapeDtypeStruct((1, tokens), jnp.float32),
        ),
        in_specs=[WHOLE] * (4 + len(parts)),
        out_specs=(WHOLE, WHOLE),
        scratch_shapes=whole,
        compiler_params=params(16),
        cost_estimate=cost(30 * experts * tokens, 12 * experts * tokens),
        name="router_terms",
    )(ids, slots, mask, policy, *parts)


def combine_kernel(parts, weights, returned, out, here, sems):
    wide = returned.shape[1] // parts
    copies = []
    for part in range(parts):
        at = pl.ds(part * wide, wide)
        value = jnp.dot(weights[...], returned[:, at], preferred_element_type=jnp.float32)
        here[:, at] = value.astype(here.dtype)
        copies.append(pltpu.make_async_copy(here.at[:, at], out.at[:, at], sems.at[part]))
        copies[part].start()
    for copy in copies:
        copy.wait()


def combine(weights, returned):
    tokens, width = weights.shape
    model_width = returned.shape[1]
    parts = 4 if model_width % 512 == 0 else 1
    return pl.pallas_call(
        functools.partial(combine_kernel, parts),
        out_shape=jax.ShapeDtypeStruct((tokens, model_width), returned.dtype),
        in_specs=[WHOLE] * 2,
        out_specs=LEFT,
        scratch_shapes=[
            pltpu.VMEM((tokens, model_width), returned.dtype),
            pltpu.SemaphoreType.DMA((parts,)),
        ],
        compiler_params=params(16),
        cost_estimate=cost(2 * tokens * width * model_width, 2 * tokens * model_width),
        name="combine",
    )(weights, returned)


def per_device(
    tokens,
    router_weight,
    gate_weight,
    up_weight,
    down_weight,
    policy_logits,
    expert_ids,
    slots,
    occupancy,
    env_mask,
):
    experts = lax.axis_size("expert")
    groups = lax.axis_size("groups")
    core = lax.axis_index("tensor")
    model_width = tokens.shape[1]
    width = experts * CAP
    staged = experts == 8 and groups == 2 and router_weight.shape[0] == 32
    ids, slots = expert_ids.T, slots.T

    hits = buffer_hits(ids, slots, width)
    outgoing = jnp.dot(hits.astype(jnp.bfloat16), tokens, preferred_element_type=jnp.float32)
    outgoing = outgoing.astype(jnp.bfloat16).reshape(experts, CAP, model_width)
    if staged:
        at, group = lax.axis_index("expert"), lax.axis_index("groups")
        mine = lax.dynamic_slice_in_dim(router_weight, core * 16, 16, axis=0)
        piece = lax.dynamic_slice_in_dim(router_weight, core * 16 + group * 8, 8, axis=0)
        blocks = {0: lax.dynamic_index_in_dim(outgoing, at, 0, keepdims=False)}
        send = {}
        for d in range(1, 8):
            block = lax.dynamic_index_in_dim(outgoing, at ^ d, 0, keepdims=False)
            along = [mine] if d in (2, 3) else [piece] if d < 5 else []
            send[d] = jnp.concatenate([block] + along, axis=0)
        for d, before in ((4, 0), (2, 0), (3, 0), (6, 0), (7, 0), (5, 4), (1, 3)):
            if before:
                blocks[before], send[d] = lax.optimization_barrier((blocks[before], send[d]))
            if d == 1:
                send[d] = jnp.concatenate([send[d], blocks[4][CAP:]], axis=0)
            blocks[d] = across(send[d], "expert", d)
        level_a = jnp.concatenate([mine] + [blocks[d][CAP : CAP + 16] for d in (2, 3)], axis=0)
        weights = (gate_weight, up_weight, down_weight)
        blocks[4], *weights = lax.optimization_barrier((blocks[4], *weights))
        held = load(*weights)
        level_b = jnp.concatenate([blocks[4][CAP:], blocks[1][2 * CAP :]], axis=0)
        level_b, *held = lax.optimization_barrier((level_b, *held))
        level_b = jnp.concatenate(
            [blocks[1][CAP : 2 * CAP], level_b, across(level_b, "expert", 2)], axis=0
        )
        arrived = jnp.concatenate([blocks[d][:CAP] for d in range(8)], axis=0)
        arrived, *held = lax.optimization_barrier((arrived, *held))
    else:
        arrived = lax.all_to_all(outgoing, "expert", split_axis=0, concat_axis=0, tiled=True)
        arrived = arrived.reshape(width, model_width)
        held = (gate_weight, up_weight, down_weight)
    ours, theirs = ffn(staged, arrived, swap_cores(arrived), occupancy, *held)
    other = swap_cores(theirs)
    if staged:
        other, level_b = lax.optimization_barrier((other, level_b))
    summed = add_halves(staged, ours, other)
    returned = lax.all_to_all(summed, "expert", split_axis=0, concat_axis=0, tiled=True)
    if staged:
        next_b = across(level_b, "groups", 1)
        peer_tokens = swap_cores(tokens)
        mine, theirs = half_logits(tokens, peer_tokens, level_a, level_b, next_b)
        parts = (mine, swap_cores(theirs))
    else:
        parts = (dot_rows(lax.all_gather(router_weight, "expert", axis=0, tiled=True), tokens),)
    weights, kl_terms = router_terms(
        ids, slots, env_mask[None, :], policy_logits.T, parts, width
    )
    return (combine(weights, returned.reshape(width, model_width)), kl_terms[0])


def solution(mesh):
    in_specs = (
        P(("groups", "expert", "tensor"), None),
        P("expert", None),
        P("expert", None, "tensor"),
        P("expert", None, "tensor"),
        P("expert", "tensor", None),
        P(("groups", "expert", "tensor"), None),
        P(("groups", "expert", "tensor"), None),
        P(("groups", "expert", "tensor"), None),
        P("expert", "groups"),
        P(("groups", "expert", "tensor")),
    )
    out_specs = (P(("groups", "expert", "tensor"), None), P(("groups", "expert", "tensor")))
    return jax.shard_map(
        per_device, mesh=mesh, in_specs=in_specs, out_specs=out_specs, check_vma=False
    )
```

```python
import functools

import jax
import jax.numpy as jnp
from jax import lax
from jax.experimental import pallas as pl
from jax.experimental.pallas import tpu as pltpu
from jax.sharding import PartitionSpec as P

CAP = 8
SWAP = [(0, 1), (1, 0)]
WHOLE = pl.BlockSpec(memory_space=pltpu.VMEM)
LEFT = pl.BlockSpec(memory_space=pltpu.HBM)


def swap_cores(value):
    return lax.ppermute(value, "tensor", SWAP)


def across(value, axis, distance):
    size = lax.axis_size(axis)
    return lax.ppermute(value, axis, [(s, s ^ distance) for s in range(size)])


def dot_rows(left, right):
    return lax.dot_general(
        left, right, (((1,), (1,)), ((), ())), preferred_element_type=jnp.float32
    )


def params(mib):
    return pltpu.CompilerParams(vmem_limit_bytes=mib << 20)


def cost(flops, nbytes):
    return pl.CostEstimate(flops=flops, bytes_accessed=nbytes, transcendentals=0)


def buffer_hits(ids, slots, width):
    choices, tokens = ids.shape
    valid = (ids < width // CAP) & (slots < CAP)
    place = jnp.where(valid, ids * CAP + slots, -1)
    rows = lax.broadcasted_iota(jnp.int32, (width, tokens), 0)
    hits = rows == place[0:1, :]
    for k in range(1, choices):
        hits = hits | (rows == place[k : k + 1, :])
    return hits


def load_kernel(*refs):
    sems = refs[-1]
    count = (len(refs) - 1) // 2
    copies = [
        pltpu.make_async_copy(refs[n], refs[count + n], sems.at[n]) for n in range(count)
    ]
    for copy in copies:
        copy.start()
    for copy in copies:
        copy.wait()


def load(*weights):
    there = [pltpu.with_memory_space_constraint(w, pltpu.HBM) for w in weights]
    return pl.pallas_call(
        load_kernel,
        out_shape=tuple(jax.ShapeDtypeStruct(w.shape, w.dtype) for w in weights),
        in_specs=[LEFT] * len(weights),
        out_specs=(WHOLE,) * len(weights),
        scratch_shapes=[pltpu.SemaphoreType.DMA((len(weights),))],
        compiler_params=params(16),
        cost_estimate=cost(0, sum(2 * w.size for w in weights)),
        name="load",
    )(*there)


def masked_hidden(g, u, occupancy, order, side):
    count = g.shape[0]
    sources = occupancy.shape[1]
    row = lax.broadcasted_iota(jnp.int32, (count, sources), 0)
    column = lax.broadcasted_iota(jnp.int32, (count, sources), 1)
    here = column == 2 * ((row // CAP) ^ order) + side
    used = jnp.sum(jnp.where(here, occupancy[...], 0), axis=1, keepdims=True)
    live = row[:, 0:1] % CAP < used
    return jnp.where(live, g / (1.0 + jnp.exp(-g)) * u, 0.0).astype(jnp.bfloat16)


def ffn_kernel(parts, relative, own, peer, occupancy, gate, up, down, out_own, out_peer):
    count = own.shape[0]
    wide = down.shape[2] // parts
    order = lax.axis_index("expert") if relative else 0
    core = lax.axis_index("tensor")
    rows = jnp.concatenate([own[...], peer[...]], axis=0)
    g = jnp.dot(rows, gate[0], preferred_element_type=jnp.float32)
    u = jnp.dot(rows, up[0], preferred_element_type=jnp.float32)
    hidden = jnp.concatenate(
        [
            masked_hidden(g[:count], u[:count], occupancy, order, core),
            masked_hidden(g[count:], u[count:], occupancy, order, 1 - core),
        ],
        axis=0,
    )
    for part in range(parts):
        at = slice(part * wide, (part + 1) * wide)
        value = jnp.dot(hidden, down[0, :, at], preferred_element_type=jnp.float32)
        value = value.astype(jnp.bfloat16)
        out_own[:, at] = value[:count]
        out_peer[:, at] = value[count:]


def ffn(relative, own, peer, occupancy, gate, up, down):
    half = jax.ShapeDtypeStruct(own.shape, own.dtype)
    count, model_width = own.shape
    hidden_width = gate.shape[2]
    parts = 4 if model_width % 512 == 0 else 1
    return pl.pallas_call(
        functools.partial(ffn_kernel, parts, relative),
        out_shape=(half, half),
        in_specs=[WHOLE] * 6,
        out_specs=(WHOLE, WHOLE),
        compiler_params=params(16),
        cost_estimate=cost(12 * count * model_width * hidden_width, 6 * model_width * hidden_width),
        name="ffn",
    )(own, peer, occupancy, gate, up, down)


def add_kernel(relative, ours, other, out, here, sems):
    value = ours[...].astype(jnp.float32) + other[...].astype(jnp.float32)
    order = lax.axis_index("expert") if relative else 0
    copies = []
    for block in range(out.shape[0]):
        here[block] = value[block * CAP : (block + 1) * CAP].astype(here.dtype)
        copies.append(
            pltpu.make_async_copy(here.at[block], out.at[block ^ order], sems.at[block])
        )
        copies[block].start()
    for copy in copies:
        copy.wait()


def add_halves(relative, ours, other):
    rows, model_width = ours.shape
    shape = (rows // CAP, CAP, model_width)
    return pl.pallas_call(
        functools.partial(add_kernel, relative),
        out_shape=jax.ShapeDtypeStruct(shape, ours.dtype),
        in_specs=[WHOLE] * 2,
        out_specs=LEFT,
        scratch_shapes=[
            pltpu.VMEM(shape, ours.dtype),
            pltpu.SemaphoreType.DMA((rows // CAP,)),
        ],
        compiler_params=params(16),
        cost_estimate=cost(ours.size, 6 * ours.size),
        name="add_halves",
    )(ours, other)


def logits_kernel(own_tokens, peer_tokens, *refs):
    levels, (out_own, out_peer) = refs[:-2], refs[-2:]
    expert, group = lax.axis_index("expert"), lax.axis_index("groups")
    rows = jnp.concatenate([level[...] for level in levels], axis=0)
    places = [(expert ^ d) * 16 for d in (0, 2)]
    for side in range(2):
        places += [(expert ^ d) * 16 + (group ^ side) * 8 for d in (1, 3, 4, 5, 6, 7)]
    for tokens, out in ((own_tokens, out_own), (peer_tokens, out_peer)):
        value = dot_rows(rows, tokens[...])
        first = 0
        for n, place in enumerate(places):
            count = 16 if n < 2 else 8
            at = pl.ds(pl.multiple_of(place, 8), count)
            out[at, :] = value[first : first + count]
            first += count


def half_logits(own_tokens, peer_tokens, *levels):
    rows = sum(level.shape[0] for level in levels)
    count, model_width = own_tokens.shape
    out = jax.ShapeDtypeStruct((rows, count), jnp.float32)
    return pl.pallas_call(
        logits_kernel,
        out_shape=(out, out),
        in_specs=[WHOLE] * (2 + len(levels)),
        out_specs=(WHOLE, WHOLE),
        compiler_params=params(16),
        cost_estimate=cost(4 * rows * count * model_width, 2 * model_width * (rows + 2 * count)),
        name="half_logits",
    )(own_tokens, peer_tokens, *levels)


def log_sigmoid(value):
    return jnp.minimum(value, 0.0) - jnp.log1p(jnp.exp(-jnp.abs(value)))


def terms_kernel(count, ids, slots, mask, policy, *refs):
    weights, kl = refs[count : count + 2]
    parts = refs[:count] + refs[count + 2 :]
    if len(parts) == 1:
        logits = parts[0][...]
    else:
        mine, theirs, whole = parts
        core = lax.axis_index("tensor")
        for block in range(mine.shape[0] // 16):
            for part, side in ((mine, core), (theirs, 1 - core)):
                at = pl.multiple_of(block * 32 + side * 16, 16)
                whole[pl.ds(at, 16), :] = part[block * 16 : (block + 1) * 16]
        logits = whole[...]
    experts, tokens = logits.shape
    width = weights.shape[1]
    window = width // CAP
    scores = 1.0 / (1.0 + jnp.exp(-logits))
    names = lax.broadcasted_iota(jnp.int32, (experts, tokens), 0)
    choices = ids[...]
    chosen = jnp.zeros((experts, tokens), jnp.float32)
    for k in range(choices.shape[0]):
        chosen = chosen + jnp.where(names == choices[k : k + 1, :], scores, 0.0)
    total = jnp.sum(chosen, axis=0, keepdims=True)
    shares = (2.5 * scores[:window] / total).astype(jnp.bfloat16).astype(jnp.float32)
    spread = jnp.broadcast_to(shares[:, None, :], (window, CAP, tokens)).reshape(width, tokens)
    hits = buffer_hits(choices, slots[...], width)
    weights[...] = jnp.where(hits, spread, 0.0).T.astype(jnp.bfloat16)
    log_p = log_sigmoid(logits) - jnp.log(jnp.sum(scores, axis=0, keepdims=True))
    q = policy[...]
    policy_scores = 1.0 / (1.0 + jnp.exp(-q))
    log_q = log_sigmoid(q) - jnp.log(jnp.sum(policy_scores, axis=0, keepdims=True))
    keep = (1 - mask[...]).astype(jnp.float32)
    kl[...] = keep * jnp.sum(jnp.exp(log_q) * (log_q - log_p), axis=0, keepdims=True)


def router_terms(ids, slots, mask, policy, parts, width):
    experts, tokens = policy.shape
    whole = [pltpu.VMEM(policy.shape, jnp.float32)] if len(parts) > 1 else []
    return pl.pallas_call(
        functools.partial(terms_kernel, len(parts)),
        out_shape=(
            jax.ShapeDtypeStruct((tokens, width), jnp.bfloat16),
            jax.ShapeDtypeStruct((1, tokens), jnp.float32),
        ),
        in_specs=[WHOLE] * (4 + len(parts)),
        out_specs=(WHOLE, WHOLE),
        scratch_shapes=whole,
        compiler_params=params(16),
        cost_estimate=cost(30 * experts * tokens, 12 * experts * tokens),
        name="router_terms",
    )(ids, slots, mask, policy, *parts)


def combine_kernel(parts, weights, returned, out, here, sems):
    wide = returned.shape[1] // parts
    copies = []
    for part in range(parts):
        at = pl.ds(part * wide, wide)
        value = jnp.dot(weights[...], returned[:, at], preferred_element_type=jnp.float32)
        here[:, at] = value.astype(here.dtype)
        copies.append(pltpu.make_async_copy(here.at[:, at], out.at[:, at], sems.at[part]))
        copies[part].start()
    for copy in copies:
        copy.wait()


def combine(weights, returned):
    tokens, width = weights.shape
    model_width = returned.shape[1]
    parts = 4 if model_width % 512 == 0 else 1
    return pl.pallas_call(
        functools.partial(combine_kernel, parts),
        out_shape=jax.ShapeDtypeStruct((tokens, model_width), returned.dtype),
        in_specs=[WHOLE] * 2,
        out_specs=LEFT,
        scratch_shapes=[
            pltpu.VMEM((tokens, model_width), returned.dtype),
            pltpu.SemaphoreType.DMA((parts,)),
        ],
        compiler_params=params(16),
        cost_estimate=cost(2 * tokens * width * model_width, 2 * tokens * model_width),
        name="combine",
    )(weights, returned)


def per_device(
    tokens,
    router_weight,
    gate_weight,
    up_weight,
    down_weight,
    policy_logits,
    expert_ids,
    slots,
    occupancy,
    env_mask,
):
    experts = lax.axis_size("expert")
    groups = lax.axis_size("groups")
    core = lax.axis_index("tensor")
    model_width = tokens.shape[1]
    width = experts * CAP
    staged = experts == 8 and groups == 2 and router_weight.shape[0] == 32
    ids, slots = expert_ids.T, slots.T

    hits = buffer_hits(ids, slots, width)
    outgoing = jnp.dot(hits.astype(jnp.bfloat16), tokens, preferred_element_type=jnp.float32)
    outgoing = outgoing.astype(jnp.bfloat16).reshape(experts, CAP, model_width)
    if staged:
        at, group = lax.axis_index("expert"), lax.axis_index("groups")
        mine = lax.dynamic_slice_in_dim(router_weight, core * 16, 16, axis=0)
        piece = lax.dynamic_slice_in_dim(router_weight, core * 16 + group * 8, 8, axis=0)
        blocks = {0: lax.dynamic_index_in_dim(outgoing, at, 0, keepdims=False)}
        send = {}
        for d in range(1, 8):
            block = lax.dynamic_index_in_dim(outgoing, at ^ d, 0, keepdims=False)
            along = [mine] if d == 2 else [piece] if d < 5 else []
            send[d] = jnp.concatenate([block] + along, axis=0)
        for d, before in ((2, 0), (4, 0), (3, 0), (7, 0), (6, 0), (5, 4), (1, 3)):
            if before:
                blocks[before], send[d] = lax.optimization_barrier((blocks[before], send[d]))
            if d == 1:
                send[d] = jnp.concatenate([send[d], blocks[4][CAP:]], axis=0)
            blocks[d] = across(send[d], "expert", d)
        level_a = jnp.concatenate([mine] + [blocks[2][CAP : CAP + 16]], axis=0)
        weights = (gate_weight, up_weight, down_weight)
        blocks[4], *weights = lax.optimization_barrier((blocks[4], *weights))
        held = load(*weights)
        level_b = jnp.concatenate([blocks[4][CAP:], blocks[1][2 * CAP :]], axis=0)
        level_b, *held = lax.optimization_barrier((level_b, *held))
        level_b = jnp.concatenate(
            [blocks[1][CAP : 2 * CAP], blocks[3][CAP:], level_b, across(level_b, "expert", 2)], axis=0
        )
        arrived = jnp.concatenate([blocks[d][:CAP] for d in range(8)], axis=0)
        arrived, *held = lax.optimization_barrier((arrived, *held))
    else:
        arrived = lax.all_to_all(outgoing, "expert", split_axis=0, concat_axis=0, tiled=True)
        arrived = arrived.reshape(width, model_width)
        held = (gate_weight, up_weight, down_weight)
    ours, theirs = ffn(staged, arrived, swap_cores(arrived), occupancy, *held)
    other = swap_cores(theirs)
    if staged:
        other, level_b = lax.optimization_barrier((other, level_b))
    summed = add_halves(staged, ours, other)
    returned = lax.all_to_all(summed, "expert", split_axis=0, concat_axis=0, tiled=True)
    if staged:
        next_b = across(level_b, "groups", 1)
        peer_tokens = swap_cores(tokens)
        mine, theirs = half_logits(tokens, peer_tokens, level_a, level_b, next_b)
        parts = (mine, swap_cores(theirs))
    else:
        parts = (dot_rows(lax.all_gather(router_weight, "expert", axis=0, tiled=True), tokens),)
    weights, kl_terms = router_terms(
        ids, slots, env_mask[None, :], policy_logits.T, parts, width
    )
    return (combine(weights, returned.reshape(width, model_width)), kl_terms[0])


def solution(mesh):
    in_specs = (
        P(("groups", "expert", "tensor"), None),
        P("expert", None),
        P("expert", None, "tensor"),
        P("expert", None, "tensor"),
        P("expert", "tensor", None),
        P(("groups", "expert", "tensor"), None),
        P(("groups", "expert", "tensor"), None),
        P(("groups", "expert", "tensor"), None),
        P("expert", "groups"),
        P(("groups", "expert", "tensor")),
    )
    out_specs = (P(("groups", "expert", "tensor"), None), P(("groups", "expert", "tensor")))
    return jax.shard_map(
        per_device, mesh=mesh, in_specs=in_specs, out_specs=out_specs, check_vma=False
    )
```

```python
import functools

import jax
import jax.numpy as jnp
from jax import lax
from jax.experimental import pallas as pl
from jax.experimental.pallas import tpu as pltpu
from jax.sharding import PartitionSpec as P

CAP = 8
SWAP = [(0, 1), (1, 0)]
WHOLE = pl.BlockSpec(memory_space=pltpu.VMEM)
LEFT = pl.BlockSpec(memory_space=pltpu.HBM)


def swap_cores(value):
    return lax.ppermute(value, "tensor", SWAP)


def across(value, axis, distance):
    size = lax.axis_size(axis)
    return lax.ppermute(value, axis, [(s, s ^ distance) for s in range(size)])


def dot_rows(left, right):
    return lax.dot_general(
        left, right, (((1,), (1,)), ((), ())), preferred_element_type=jnp.float32
    )


def params(mib):
    return pltpu.CompilerParams(vmem_limit_bytes=mib << 20)


def cost(flops, nbytes):
    return pl.CostEstimate(flops=flops, bytes_accessed=nbytes, transcendentals=0)


def buffer_hits(ids, slots, width):
    choices, tokens = ids.shape
    valid = (ids < width // CAP) & (slots < CAP)
    place = jnp.where(valid, ids * CAP + slots, -1)
    rows = lax.broadcasted_iota(jnp.int32, (width, tokens), 0)
    hits = rows == place[0:1, :]
    for k in range(1, choices):
        hits = hits | (rows == place[k : k + 1, :])
    return hits


def load_kernel(*refs):
    sems = refs[-1]
    count = (len(refs) - 1) // 2
    copies = [
        pltpu.make_async_copy(refs[n], refs[count + n], sems.at[n]) for n in range(count)
    ]
    for copy in copies:
        copy.start()
    for copy in copies:
        copy.wait()


def load(*weights):
    there = [pltpu.with_memory_space_constraint(w, pltpu.HBM) for w in weights]
    return pl.pallas_call(
        load_kernel,
        out_shape=tuple(jax.ShapeDtypeStruct(w.shape, w.dtype) for w in weights),
        in_specs=[LEFT] * len(weights),
        out_specs=(WHOLE,) * len(weights),
        scratch_shapes=[pltpu.SemaphoreType.DMA((len(weights),))],
        compiler_params=params(16),
        cost_estimate=cost(0, sum(2 * w.size for w in weights)),
        name="load",
    )(*there)


def masked_hidden(g, u, occupancy, order, side):
    count = g.shape[0]
    sources = occupancy.shape[1]
    row = lax.broadcasted_iota(jnp.int32, (count, sources), 0)
    column = lax.broadcasted_iota(jnp.int32, (count, sources), 1)
    here = column == 2 * ((row // CAP) ^ order) + side
    used = jnp.sum(jnp.where(here, occupancy[...], 0), axis=1, keepdims=True)
    live = row[:, 0:1] % CAP < used
    return jnp.where(live, g / (1.0 + jnp.exp(-g)) * u, 0.0).astype(jnp.bfloat16)


def ffn_kernel(parts, relative, own, peer, occupancy, gate, up, down, out_own, out_peer):
    count = own.shape[0]
    wide = down.shape[2] // parts
    order = lax.axis_index("expert") if relative else 0
    core = lax.axis_index("tensor")
    rows = jnp.concatenate([own[...], peer[...]], axis=0)
    g = jnp.dot(rows, gate[0], preferred_element_type=jnp.float32)
    u = jnp.dot(rows, up[0], preferred_element_type=jnp.float32)
    hidden = jnp.concatenate(
        [
            masked_hidden(g[:count], u[:count], occupancy, order, core),
            masked_hidden(g[count:], u[count:], occupancy, order, 1 - core),
        ],
        axis=0,
    )
    for part in range(parts):
        at = slice(part * wide, (part + 1) * wide)
        value = jnp.dot(hidden, down[0, :, at], preferred_element_type=jnp.float32)
        value = value.astype(jnp.bfloat16)
        out_own[:, at] = value[:count]
        out_peer[:, at] = value[count:]


def ffn(relative, own, peer, occupancy, gate, up, down):
    half = jax.ShapeDtypeStruct(own.shape, own.dtype)
    count, model_width = own.shape
    hidden_width = gate.shape[2]
    parts = 4 if model_width % 512 == 0 else 1
    return pl.pallas_call(
        functools.partial(ffn_kernel, parts, relative),
        out_shape=(half, half),
        in_specs=[WHOLE] * 6,
        out_specs=(WHOLE, WHOLE),
        compiler_params=params(16),
        cost_estimate=cost(12 * count * model_width * hidden_width, 6 * model_width * hidden_width),
        name="ffn",
    )(own, peer, occupancy, gate, up, down)


def add_kernel(relative, ours, other, out, here, sems):
    value = ours[...].astype(jnp.float32) + other[...].astype(jnp.float32)
    order = lax.axis_index("expert") if relative else 0
    copies = []
    for block in range(out.shape[0]):
        here[block] = value[block * CAP : (block + 1) * CAP].astype(here.dtype)
        copies.append(
            pltpu.make_async_copy(here.at[block], out.at[block ^ order], sems.at[block])
        )
        copies[block].start()
    for copy in copies:
        copy.wait()


def add_halves(relative, ours, other):
    rows, model_width = ours.shape
    shape = (rows // CAP, CAP, model_width)
    return pl.pallas_call(
        functools.partial(add_kernel, relative),
        out_shape=jax.ShapeDtypeStruct(shape, ours.dtype),
        in_specs=[WHOLE] * 2,
        out_specs=LEFT,
        scratch_shapes=[
            pltpu.VMEM(shape, ours.dtype),
            pltpu.SemaphoreType.DMA((rows // CAP,)),
        ],
        compiler_params=params(16),
        cost_estimate=cost(ours.size, 6 * ours.size),
        name="add_halves",
    )(ours, other)


def logits_kernel(own_tokens, peer_tokens, *refs):
    levels, (out_own, out_peer) = refs[:-2], refs[-2:]
    expert, group = lax.axis_index("expert"), lax.axis_index("groups")
    rows = jnp.concatenate([level[...] for level in levels], axis=0)
    places = [(expert ^ d) * 16 for d in (0, 2)]
    for side in range(2):
        places += [(expert ^ d) * 16 + (group ^ side) * 8 for d in (1, 3, 4, 5, 6, 7)]
    for tokens, out in ((own_tokens, out_own), (peer_tokens, out_peer)):
        value = dot_rows(rows, tokens[...])
        first = 0
        for n, place in enumerate(places):
            count = 16 if n < 2 else 8
            at = pl.ds(pl.multiple_of(place, 8), count)
            out[at, :] = value[first : first + count]
            first += count


def half_logits(own_tokens, peer_tokens, *levels):
    rows = sum(level.shape[0] for level in levels)
    count, model_width = own_tokens.shape
    out = jax.ShapeDtypeStruct((rows, count), jnp.float32)
    return pl.pallas_call(
        logits_kernel,
        out_shape=(out, out),
        in_specs=[WHOLE] * (2 + len(levels)),
        out_specs=(WHOLE, WHOLE),
        compiler_params=params(16),
        cost_estimate=cost(4 * rows * count * model_width, 2 * model_width * (rows + 2 * count)),
        name="half_logits",
    )(own_tokens, peer_tokens, *levels)


def log_sigmoid(value):
    return jnp.minimum(value, 0.0) - jnp.log1p(jnp.exp(-jnp.abs(value)))


def terms_kernel(count, ids, slots, mask, policy, *refs):
    weights, kl = refs[count : count + 2]
    parts = refs[:count] + refs[count + 2 :]
    if len(parts) == 1:
        logits = parts[0][...]
    else:
        mine, theirs, whole = parts
        core = lax.axis_index("tensor")
        for block in range(mine.shape[0] // 16):
            for part, side in ((mine, core), (theirs, 1 - core)):
                at = pl.multiple_of(block * 32 + side * 16, 16)
                whole[pl.ds(at, 16), :] = part[block * 16 : (block + 1) * 16]
        logits = whole[...]
    experts, tokens = logits.shape
    width = weights.shape[1]
    window = width // CAP
    scores = 1.0 / (1.0 + jnp.exp(-logits))
    names = lax.broadcasted_iota(jnp.int32, (experts, tokens), 0)
    choices = ids[...]
    chosen = jnp.zeros((experts, tokens), jnp.float32)
    for k in range(choices.shape[0]):
        chosen = chosen + jnp.where(names == choices[k : k + 1, :], scores, 0.0)
    total = jnp.sum(chosen, axis=0, keepdims=True)
    shares = (2.5 * scores[:window] / total).astype(jnp.bfloat16).astype(jnp.float32)
    spread = jnp.broadcast_to(shares[:, None, :], (window, CAP, tokens)).reshape(width, tokens)
    hits = buffer_hits(choices, slots[...], width)
    weights[...] = jnp.where(hits, spread, 0.0).T.astype(jnp.bfloat16)
    log_p = log_sigmoid(logits) - jnp.log(jnp.sum(scores, axis=0, keepdims=True))
    q = policy[...]
    policy_scores = 1.0 / (1.0 + jnp.exp(-q))
    log_q = log_sigmoid(q) - jnp.log(jnp.sum(policy_scores, axis=0, keepdims=True))
    keep = (1 - mask[...]).astype(jnp.float32)
    kl[...] = keep * jnp.sum(jnp.exp(log_q) * (log_q - log_p), axis=0, keepdims=True)


def router_terms(ids, slots, mask, policy, parts, width):
    experts, tokens = policy.shape
    whole = [pltpu.VMEM(policy.shape, jnp.float32)] if len(parts) > 1 else []
    return pl.pallas_call(
        functools.partial(terms_kernel, len(parts)),
        out_shape=(
            jax.ShapeDtypeStruct((tokens, width), jnp.bfloat16),
            jax.ShapeDtypeStruct((1, tokens), jnp.float32),
        ),
        in_specs=[WHOLE] * (4 + len(parts)),
        out_specs=(WHOLE, WHOLE),
        scratch_shapes=whole,
        compiler_params=params(16),
        cost_estimate=cost(30 * experts * tokens, 12 * experts * tokens),
        name="router_terms",
    )(ids, slots, mask, policy, *parts)


def combine_kernel(parts, weights, returned, out, here, sems):
    wide = returned.shape[1] // parts
    copies = []
    for part in range(parts):
        at = pl.ds(part * wide, wide)
        value = jnp.dot(weights[...], returned[:, at], preferred_element_type=jnp.float32)
        here[:, at] = value.astype(here.dtype)
        copies.append(pltpu.make_async_copy(here.at[:, at], out.at[:, at], sems.at[part]))
        copies[part].start()
    for copy in copies:
        copy.wait()


def combine(weights, returned):
    tokens, width = weights.shape
    model_width = returned.shape[1]
    parts = 4 if model_width % 512 == 0 else 1
    return pl.pallas_call(
        functools.partial(combine_kernel, parts),
        out_shape=jax.ShapeDtypeStruct((tokens, model_width), returned.dtype),
        in_specs=[WHOLE] * 2,
        out_specs=LEFT,
        scratch_shapes=[
            pltpu.VMEM((tokens, model_width), returned.dtype),
            pltpu.SemaphoreType.DMA((parts,)),
        ],
        compiler_params=params(16),
        cost_estimate=cost(2 * tokens * width * model_width, 2 * tokens * model_width),
        name="combine",
    )(weights, returned)


def per_device(
    tokens,
    router_weight,
    gate_weight,
    up_weight,
    down_weight,
    policy_logits,
    expert_ids,
    slots,
    occupancy,
    env_mask,
):
    experts = lax.axis_size("expert")
    groups = lax.axis_size("groups")
    core = lax.axis_index("tensor")
    model_width = tokens.shape[1]
    width = experts * CAP
    staged = experts == 8 and groups == 2 and router_weight.shape[0] == 32
    ids, slots = expert_ids.T, slots.T

    hits = buffer_hits(ids, slots, width)
    outgoing = jnp.dot(hits.astype(jnp.bfloat16), tokens, preferred_element_type=jnp.float32)
    outgoing = outgoing.astype(jnp.bfloat16).reshape(experts, CAP, model_width)
    if staged:
        at, group = lax.axis_index("expert"), lax.axis_index("groups")
        mine = lax.dynamic_slice_in_dim(router_weight, core * 16, 16, axis=0)
        piece = lax.dynamic_slice_in_dim(router_weight, core * 16 + group * 8, 8, axis=0)
        blocks = {0: lax.dynamic_index_in_dim(outgoing, at, 0, keepdims=False)}
        send = {}
        for d in range(1, 8):
            block = lax.dynamic_index_in_dim(outgoing, at ^ d, 0, keepdims=False)
            along = [mine] if d == 2 else [piece] if d < 5 else []
            send[d] = jnp.concatenate([block] + along, axis=0)
        for d, before in ((4, 0), (2, 0), (3, 0), (6, 0), (7, 0), (5, 4), (1, 3)):
            if before:
                blocks[before], send[d] = lax.optimization_barrier((blocks[before], send[d]))
            if d == 1:
                send[d] = jnp.concatenate([send[d], blocks[4][CAP:]], axis=0)
            blocks[d] = across(send[d], "expert", d)
        level_a = jnp.concatenate([mine] + [blocks[2][CAP : CAP + 16]], axis=0)
        weights = (gate_weight, up_weight, down_weight)
        blocks[4], *weights = lax.optimization_barrier((blocks[4], *weights))
        held = load(*weights)
        level_b = jnp.concatenate([blocks[4][CAP:], blocks[1][2 * CAP :]], axis=0)
        level_b, *held = lax.optimization_barrier((level_b, *held))
        level_b = jnp.concatenate(
            [blocks[1][CAP : 2 * CAP], blocks[3][CAP:], level_b, across(level_b, "expert", 2)], axis=0
        )
        arrived = jnp.concatenate([blocks[d][:CAP] for d in range(8)], axis=0)
        arrived, *held = lax.optimization_barrier((arrived, *held))
    else:
        arrived = lax.all_to_all(outgoing, "expert", split_axis=0, concat_axis=0, tiled=True)
        arrived = arrived.reshape(width, model_width)
        held = (gate_weight, up_weight, down_weight)
    ours, theirs = ffn(staged, arrived, swap_cores(arrived), occupancy, *held)
    other = swap_cores(theirs)
    if staged:
        other, level_b = lax.optimization_barrier((other, level_b))
    summed = add_halves(staged, ours, other)
    returned = lax.all_to_all(summed, "expert", split_axis=0, concat_axis=0, tiled=True)
    if staged:
        next_b = across(level_b, "groups", 1)
        peer_tokens = swap_cores(tokens)
        mine, theirs = half_logits(tokens, peer_tokens, level_a, level_b, next_b)
        parts = (mine, swap_cores(theirs))
    else:
        parts = (dot_rows(lax.all_gather(router_weight, "expert", axis=0, tiled=True), tokens),)
    weights, kl_terms = router_terms(
        ids, slots, env_mask[None, :], policy_logits.T, parts, width
    )
    return (combine(weights, returned.reshape(width, model_width)), kl_terms[0])


def solution(mesh):
    in_specs = (
        P(("groups", "expert", "tensor"), None),
        P("expert", None),
        P("expert", None, "tensor"),
        P("expert", None, "tensor"),
        P("expert", "tensor", None),
        P(("groups", "expert", "tensor"), None),
        P(("groups", "expert", "tensor"), None),
        P(("groups", "expert", "tensor"), None),
        P("expert", "groups"),
        P(("groups", "expert", "tensor")),
    )
    out_specs = (P(("groups", "expert", "tensor"), None), P(("groups", "expert", "tensor")))
    return jax.shard_map(
        per_device, mesh=mesh, in_specs=in_specs, out_specs=out_specs, check_vma=False
    )
```
